512 devices in a mesh: tile: 64 (over z, x_hi, core), lev: 8 (over x_lo, y).
Axes of the slice: x: 4 (x_hi: 2, x_lo: 2; x = x_hi * 2 + x_lo), y: 4, z: 16, core: 2. Of those that a mesh axis runs over, the one named last changes fastest.
Arguments:
- pre_act: bfloat16 [64, 8, 64, 2304], P('tile', 'lev'), may hold values from -6 to 6
- cotangent: bfloat16 [64, 8, 2304], P('tile', 'lev'), may hold values from -6 to 6
- input_weight: bfloat16 [9, 64, 2], replicated, may hold values from -0.75 to 0.75
- conv_weight: bfloat16 [9, 64, 64], replicated, may hold values from -0.25 to 0.25
- down_weight: bfloat16 [8, 64], replicated, may hold values from -0.75 to 0.75
- level_mix: float32 [8, 8], replicated, may hold values from -2 to 2
- up_weight: bfloat16 [64, 8], replicated, may hold values from -2 to 2
- head_weight: float32 [64], replicated, may hold values from -8 to 8
- seam_list: int32 [64, 4, 3], replicated, may hold values from 0 to 63, as said below
- tile_panel: int32 [64], replicated, may hold values from 0 to 6, as said below
Outputs:
- sensitivity: float32 [64, 8, 2, 2304], P('tile', 'lev')
The draws below stay inside these ranges and needn't reach their ends.
Inputs may be any that keep to these rules, and one draw needn't show every extreme that they name: seam_list[t, d] = (p, e, q): edge e of the tile on device p lies along side d of the tile on device t (0 start of rows, 1 end of rows, 2 start of columns, 3 end of columns), q = 1 where positions along the seam run opposite ways; the relation is symmetric, seam_list[p, e] = (t, d, q). The 54 tiles are the 3 x 3 tiles of each face of a cube, placed on devices in an order drawn from the seed; a device with no tile lists itself with edge d for side d and q = 0. `tile_panel`: panel of the tile held by each device, 6 where the device holds no tile; it agrees with seam_list.
All inputs are finite; a program needn't handle non-finite values.
Results may differ from the reference program's by a relative error of at most 0.0075.
Values may be sent and summed in bfloat16 or wider, within the bound.
A program may use at most 64 MiB of HBM per device.

```python
import jax
import jax.numpy as jnp
import numpy as np
from jax import lax

TS = 48
HID = 64
ZC = 8
C_IN = 8
R1 = 4
R2 = 8
S = 3
LEVELS = 8
TSQ = 2304
N_TILE = 64


PANEL_SIDES = np.array([[[4, 1, 0], [5, 0, 0], [3, 3, 0], [1, 2, 0]], [[4, 3, 1], [5, 3, 0], [0, 3, 0], [2, 2, 0]], [[4, 0, 1], [5, 1, 1], [1, 3, 0], [3, 2, 0]], [[4, 2, 0], [5, 2, 1], [2, 3, 0], [0, 2, 0]], [[2, 0, 1], [0, 0, 0], [3, 0, 0], [1, 0, 1]], [[0, 1, 0], [2, 1, 1], [3, 1, 1], [1, 1, 0]]], np.int32)


def tile_neighbours(across):
    per_panel = across * across
    result = np.zeros((6 * per_panel, 4, 3), np.int32)
    for panel_id in range(6):
        for row_id in range(across):
            for col_id in range(across):
                square = panel_id * per_panel + row_id * across + col_id
                inside = [(row_id - 1, col_id, 1), (row_id + 1, col_id, 0), (row_id, col_id - 1, 3), (row_id, col_id + 1, 2)]
                for side_id in range(4):
                    near_row, near_col, facing = inside[side_id]
                    if 0 <= near_row < across and 0 <= near_col < across:
                        result[square, side_id] = (panel_id * per_panel + near_row * across + near_col, facing, 0)
                    else:
                        other_panel = int(PANEL_SIDES[panel_id, side_id, 0])
                        facing = int(PANEL_SIDES[panel_id, side_id, 1])
                        reverse = int(PANEL_SIDES[panel_id, side_id, 2])
                        position = col_id if side_id < 2 else row_id
                        if reverse:
                            position = across - 1 - position
                        landing = [(0, position), (across - 1, position), (position, 0), (position, across - 1)]
                        near_row, near_col = landing[facing]
                        result[square, side_id] = (other_panel * per_panel + near_row * across + near_col, facing, reverse)
    return result


def holders(key):
    placing = jax.random.permutation(jax.random.fold_in(key, 7), N_TILE).astype(jnp.int32)
    holder = jnp.argsort(placing).astype(jnp.int32)
    return (placing, holder)


def draw_seam_list(key, part):
    placing, holder = holders(key)
    neighbours = jnp.asarray(tile_neighbours(S))
    tile_count = 6 * S * S
    active = (holder < tile_count)[:, None]
    entries = neighbours[jnp.minimum(holder, tile_count - 1)]
    peer_device = placing[entries[:, :, 0]]
    itself = jnp.broadcast_to(jnp.arange(N_TILE, dtype=jnp.int32)[:, None], (N_TILE, 4))
    side_ids = jnp.broadcast_to(jnp.arange(4, dtype=jnp.int32)[None, :], (N_TILE, 4))
    stacked = jnp.stack([jnp.where(active, peer_device, itself), jnp.where(active, entries[:, :, 1], side_ids), jnp.where(active, entries[:, :, 2], 0)], axis=-1)
    return stacked.astype(jnp.int32)


def draw_tile_panel(key, part):
    placing, holder = holders(key)
    tile_count = 6 * S * S
    return jnp.where(holder < tile_count, holder // (S * S), 6).astype(jnp.int32)


def block_levels(own_key, shape, pieces, smallest, top_value):
    factor_of = 1.0
    for dim, parts in pieces:
        draws = jax.random.uniform(jax.random.fold_in(jax.random.fold_in(own_key, 6), dim), (parts,), jnp.float32, smallest / len(pieces), top_value / len(pieces))
        factor_of = factor_of * jnp.repeat(jnp.exp(draws), shape[dim] // parts).reshape((-1,) + (1,) * (len(shape) - 1 - dim))
    return factor_of


def bell_draw(own_key, dims, scale, limit, split=(), kind=jnp.bfloat16):
    values = jax.random.normal(own_key, dims, jnp.float32) * scale
    if len(split) > 0:
        values = block_levels(own_key, dims, split, -0.22, 0.18) * values
    return jnp.clip(values, min=-limit, max=limit).astype(kind)


def setup_inputs(seed: int = 0) -> dict:
    keys = jax.random.split(jax.random.key(seed), 11)
    pre_act = bell_draw(keys[0], (N_TILE, LEVELS, HID, TSQ), 1.5, 6.0, ((0, 64), (1, 8)))
    cotangent = bell_draw(keys[1], (N_TILE, LEVELS, TSQ), 1.0, 6.0, ((0, 64), (1, 8)))
    input_weight = bell_draw(keys[2], (9, HID, 2), (9 * C_IN) ** -0.5, 0.75)
    conv_weight = bell_draw(keys[3], (9, HID, HID), (9 * HID) ** -0.5, 0.25)
    down_weight = bell_draw(keys[4], (ZC, HID), HID ** -0.5, 0.75)
    level_mix = bell_draw(keys[5], (LEVELS, LEVELS), LEVELS ** -0.5, 2.0, (), jnp.float32)
    up_weight = bell_draw(keys[6], (HID, ZC), ZC ** -0.5, 2.0)
    head_weight = bell_draw(keys[7], (HID,), 2.0, 8.0, (), jnp.float32)
    seam_list = draw_seam_list(jax.random.fold_in(keys[10], 71), 0)
    tile_panel = draw_tile_panel(jax.random.fold_in(keys[10], 71), 0)
    return {"pre_act": pre_act, "cotangent": cotangent, "input_weight": input_weight, "conv_weight": conv_weight, "down_weight": down_weight, "level_mix": level_mix, "up_weight": up_weight, "head_weight": head_weight, "seam_list": seam_list, "tile_panel": tile_panel}


def widen(values):
    return lax.optimization_barrier(values).astype(jnp.float32)

def silu_grad(values):
    logistic = jax.nn.sigmoid(values)
    return logistic * (1.0 + values * (1.0 - logistic))

def edge_strips(square, rim_depth):
    upper_band = square[:, :rim_depth, :]
    lower_band = jnp.flip(square[:, -rim_depth:, :], axis=1)
    left_band = jnp.swapaxes(square[:, :, :rim_depth], 1, 2)
    right_band = jnp.flip(jnp.swapaxes(square[:, :, -rim_depth:], 1, 2), axis=1)
    return jnp.stack([upper_band, lower_band, left_band, right_band])

def orient(strips, reversal):
    turned = jnp.flip(strips, axis=3)
    return jnp.where(reversal[:, None, None, None] > 0, turned, strips)

def assemble(square, rims, rim_depth):
    channels = square.shape[0]
    upper_band = jnp.flip(rims[0], axis=1)
    left_band = jnp.swapaxes(jnp.flip(rims[2], axis=1), 1, 2)
    right_band = jnp.swapaxes(rims[3], 1, 2)
    middle = jnp.concatenate([left_band, square, right_band], axis=2)
    corner = jnp.zeros((channels, rim_depth, rim_depth), square.dtype)
    upper_rows = jnp.concatenate([corner, upper_band, corner], axis=2)
    lower_rows = jnp.concatenate([corner, rims[1], corner], axis=2)
    return jnp.concatenate([upper_rows, middle, lower_rows], axis=1)

def unassemble(joined, rim_depth, reversal):
    extent = joined.shape[1] - 2 * rim_depth
    far = rim_depth + extent
    interior = joined[:, rim_depth:far, rim_depth:far]
    upper_band = jnp.flip(joined[:, :rim_depth, rim_depth:far], axis=1)
    lower_band = joined[:, far:, rim_depth:far]
    left_band = jnp.flip(jnp.swapaxes(joined[:, rim_depth:far, :rim_depth], 1, 2), axis=1)
    right_band = jnp.swapaxes(joined[:, rim_depth:far, far:], 1, 2)
    borders = orient(jnp.stack([upper_band, lower_band, left_band, right_band]), reversal).astype(jnp.bfloat16)
    return (interior, borders)

def add_edges(interior, borders):
    extent = interior.shape[1]
    rim_depth = borders.shape[2]
    rest = extent - rim_depth
    upper_band = jnp.pad(borders[0], ((0, 0), (0, rest), (0, 0)))
    lower_band = jnp.pad(jnp.flip(borders[1], axis=1), ((0, 0), (rest, 0), (0, 0)))
    left_band = jnp.pad(jnp.swapaxes(borders[2], 1, 2), ((0, 0), (0, 0), (0, rest)))
    right_band = jnp.pad(jnp.swapaxes(jnp.flip(borders[3], axis=1), 1, 2), ((0, 0), (0, 0), (rest, 0)))
    return interior + upper_band + lower_band + left_band + right_band

def pad_tiles(squares, rim_depth, seam_list):
    strips = jax.vmap(lambda square: edge_strips(square, rim_depth))(squares)
    fetched = strips[seam_list[:, :, 0], seam_list[:, :, 1]]
    return jax.vmap(lambda square, rims, reversal: assemble(square, orient(rims, reversal), rim_depth))(squares, fetched, seam_list[:, :, 2])

def unpad_tiles(joined, rim_depth, seam_list):
    interior, borders = jax.vmap(lambda field, reversal: unassemble(field, rim_depth, reversal))(joined, seam_list[:, :, 2])
    fetched = widen(borders[seam_list[:, :, 0], seam_list[:, :, 1]])
    return jax.vmap(add_edges)(interior, fetched)

def conv_tiles(padded, weight, spacing):
    kernel = weight.astype(jnp.float32).reshape(3, 3, weight.shape[1], weight.shape[2]).transpose(2, 3, 0, 1)
    return lax.conv_general_dilated(padded, kernel, (1, 1), 'VALID', rhs_dilation=(spacing, spacing), dimension_numbers=('NCHW', 'OIHW', 'NCHW'), precision=lax.Precision.HIGHEST)

def conv_adjoint(grads, weight, spacing):
    grid_shape = (grads.shape[0], weight.shape[2], TS + 2 * spacing, TS + 2 * spacing)
    unused, pullback = jax.vjp(lambda field: conv_tiles(field, weight, spacing), jnp.zeros(grid_shape, jnp.float32))
    return pullback(grads)[0]

def reference(pre_act, cotangent, input_weight, conv_weight, down_weight, level_mix, up_weight, head_weight, seam_list, tile_panel):
    levels = jnp.arange(pre_act.shape[1])
    squares_count = pre_act.shape[0]

    def level_slice(values, level_index):
        return lax.dynamic_index_in_dim(values, level_index, 1, keepdims=False)

    def forward_level(level_index):
        pre_level = level_slice(pre_act, level_index)
        first_act = jax.nn.silu(pre_level.astype(jnp.float32)).astype(jnp.bfloat16)
        padded = pad_tiles(first_act.reshape(squares_count, HID, TS, TS), R2, seam_list)
        second_pre = conv_tiles(widen(padded), conv_weight, R2).reshape(squares_count, HID, TS * TS)
        second_act = jax.nn.silu(second_pre).astype(jnp.bfloat16)
        latents = jnp.einsum('zh,nhc->nzc', down_weight.astype(jnp.float32), widen(second_act), precision=lax.Precision.HIGHEST).astype(jnp.bfloat16)
        return (second_pre, second_act, latents)
    latents = lax.map(lambda level_index: forward_level(level_index)[2], levels)
    mixture = jnp.einsum('ml,lnzc->mnzc', level_mix, widen(latents), precision=lax.Precision.HIGHEST).astype(jnp.bfloat16)

    def head_level(level_index):
        second_pre, second_act, unused = forward_level(level_index)
        mixed_here = widen(lax.dynamic_index_in_dim(mixture, level_index, 0, keepdims=False))
        third_act = widen(second_act) + jnp.einsum('hz,nzc->nhc', up_weight.astype(jnp.float32), mixed_here, precision=lax.Precision.HIGHEST)
        top_grad = level_slice(cotangent, level_index).astype(jnp.float32)[:, None, :] * head_weight[None, :, None] * silu_grad(third_act)
        return (second_pre, top_grad)

    def grad_latents(level_index):
        unused, top_grad = head_level(level_index)
        top_half = widen(top_grad.astype(jnp.bfloat16))
        return jnp.einsum('hz,nhc->nzc', up_weight.astype(jnp.float32), top_half, precision=lax.Precision.HIGHEST).astype(jnp.bfloat16)
    latent_grad = lax.map(grad_latents, levels)
    mixed_grad = jnp.einsum('lm,lnzc->mnzc', level_mix, widen(latent_grad), precision=lax.Precision.HIGHEST).astype(jnp.bfloat16)

    def backward_level(level_index):
        second_pre, top_grad = head_level(level_index)
        mixed_here = widen(lax.dynamic_index_in_dim(mixed_grad, level_index, 0, keepdims=False))
        second_grad = top_grad + jnp.einsum('zh,nzc->nhc', down_weight.astype(jnp.float32), mixed_here, precision=lax.Precision.HIGHEST)
        deep_grad = (second_grad * silu_grad(second_pre)).astype(jnp.bfloat16)
        padded_grad = conv_adjoint(widen(deep_grad).reshape(squares_count, HID, TS, TS), conv_weight, R2)
        first_grad = unpad_tiles(padded_grad, R2, seam_list).reshape(squares_count, HID, TS * TS)
        pre_wide = level_slice(pre_act, level_index).astype(jnp.float32)
        shallow_grad = (first_grad * silu_grad(pre_wide)).astype(jnp.bfloat16)
        input_grad = conv_adjoint(widen(shallow_grad).reshape(squares_count, HID, TS, TS), input_weight, R1)
        return unpad_tiles(input_grad, R1, seam_list).reshape(squares_count, 2, TS * TS)
    result = lax.map(backward_level, levels)
    active = (tile_panel < 6).astype(jnp.float32)
    return jnp.transpose(result, (1, 0, 2, 3)) * active[:, None, None, None]
```

```python
import functools

import jax
import jax.numpy as jnp
from jax import lax
from jax.experimental import pallas as pl
from jax.experimental.pallas import tpu as pltpu
from jax.sharding import PartitionSpec as P

F32 = jnp.float32
BF16 = jnp.bfloat16
MESH = pl.DeviceIdType.MESH
NT = (((1,), (1,)), ((), ()))
NN = (((1,), (0,)), ((), ()))
TILES = 64
LEVS = 8


def dot(a, b, dims=NN):
    return lax.dot_general(a, b, dims, preferred_element_type=F32)


def dsilu(v):
    g = jax.nn.sigmoid(v)
    return g * (1.0 + v * (1.0 - g))


def iota(shape, axis):
    return lax.broadcasted_iota(jnp.int32, shape, axis)


def rows_from_pieces(rows, pieces):
    view = rows.reshape(3, 32, 8, 128)

    def step(m, carry):
        for h in range(2):
            for j in range(3):
                view[j, m, 4 * h : 4 * h + 4, :] = pieces[2 * m + h, j].astype(F32)
        return carry

    lax.fori_loop(0, 32, step, 0)


def pieces_from_rows(pieces, rows):
    view = rows.reshape(3, 32, 8, 128)

    def step(m, carry):
        for h in range(2):
            for j in range(3):
                pieces[2 * m + h, j] = view[j, m, 4 * h : 4 * h + 4, :].astype(BF16)
        return carry

    lax.fori_loop(0, 32, step, 0)


def rows_from_slab(rows, member, slab):
    for j in range(3):
        block = jnp.concatenate([slab[128 * j : 128 * j + 64], slab[128 * j + 64 : 128 * j + 128]], axis=1)
        rows[j, pl.ds(member, 64, stride=4), :] = block


def slab_from_rows(rows, member):
    parts = []
    for j in range(3):
        block = rows[j, pl.ds(member, 64, stride=4), :]
        parts += [block[:, :64], block[:, 64:]]
    return jnp.concatenate(parts, axis=0)


def spread_start(send, recv, send_sem, recv_sem, me):
    recv[me] = send[me]

    def step(i, carry):
        target = lax.rem(me + i, TILES)
        pltpu.make_async_remote_copy(
            send.at[target], recv.at[me], send_sem, recv_sem,
            device_id={"tile": target}, device_id_type=MESH,
        ).start()
        return carry

    lax.fori_loop(1, TILES, step, 0)


def spread_wait(send, recv, send_sem, recv_sem):
    others = pl.ds(0, TILES - 1)
    pltpu.make_async_copy(recv.at[others], recv.at[others], recv_sem).wait()
    pltpu.make_async_copy(send.at[others], send.at[others], send_sem).wait()


def level_start(buf, send_sem, recv_sem, level):
    for i in range(1, LEVS):
        pltpu.make_async_remote_copy(
            buf.at[level], buf.at[level], send_sem, recv_sem,
            device_id={"lev": lax.rem(level + i, LEVS)}, device_id_type=MESH,
        ).start()


def level_wait(buf, send_sem, recv_sem):
    others = pl.ds(0, LEVS - 1)
    pltpu.make_async_copy(buf.at[others], buf.at[others], recv_sem).wait()
    pltpu.make_async_copy(buf.at[others], buf.at[others], send_sem).wait()


def pick(rows, choice):
    for j in range(3):
        rows[j] = dot(choice, rows[j].astype(BF16))


def turn_matrix(side, edge, flip, of_bands):
    if side < 2:
        r, b = iota((8, 48, 128), 0), iota((8, 48, 128), 1)
    else:
        b, r = iota((48, 8, 128), 0), iota((48, 8, 128), 1)
    r, b = r.reshape(384, 128), b.reshape(384, 128)
    turned_here = (side % 2 == 0) if not of_bands else (side % 2 == 1)
    a = 7 - r if turned_here else r
    odd = lax.rem(edge, 2)
    turned_there = odd if not of_bands else 1 - odd
    depth = turned_there * 7 + (1 - 2 * turned_there) * a
    along = flip * 47 + (1 - 2 * flip) * b
    by_rows = jnp.where(edge < 2, 1, 0)
    index = depth * (1 + 47 * by_rows) + along * (8 - 7 * by_rows)
    lanes = iota((384, 128), 1)
    return jnp.concatenate(
        [jnp.where(index == lanes + 128 * j, 1.0, 0.0).astype(BF16) for j in range(3)], axis=1
    )


def kernel(
    pre_ref, cot_ref, in_w, conv_w, down_ref, mix_ref, up_ref, head_ref, seam, seam_v, panel, out_ref,
    pre_t, padded, wide, act, second, top, deep_wide, grad, shallow, bands_t, turns, place, rows, wanted,
    choice, a_send, a_recv, b_send, b_recv, c_send, c_recv, d_send, d_recv, e_send, e_recv, lat, glat,
    send_sem, recv_sem,
):
    me = lax.axis_index("tile")
    level = lax.axis_index("lev")
    barrier = pltpu.get_barrier_semaphore()

    def greet(i, carry):
        pl.semaphore_signal(barrier, inc=1, device_id={"tile": lax.rem(me + i, TILES)}, device_id_type=MESH)
        return carry

    lax.fori_loop(1, TILES, greet, 0)
    for i in range(1, LEVS):
        pl.semaphore_signal(barrier, inc=1, device_id={"lev": lax.rem(level + i, LEVS)}, device_id_type=MESH)

    pre_t[...] = pre_ref[0, 0].astype(F32).T.reshape(48, 48, 64)
    padded[0:8] = jnp.zeros((8, 64, 64), F32)
    padded[56:64] = jnp.zeros((8, 64, 64), F32)

    def first(c, carry):
        v = pre_t[pl.ds(8 * c, 8)]
        s = v * jax.nn.sigmoid(v)
        padded[pl.ds(8 * c + 8, 8), 8:56, :] = s.astype(BF16).astype(F32)
        return carry

    lax.fori_loop(0, 6, first, 0)
    rows_from_slab(rows, 0, padded[8:16, 8:56, :].reshape(384, 64))
    rows_from_slab(rows, 1, padded[48:56, 8:56, :].reshape(384, 64))
    rows_from_slab(rows, 2, padded[8:56, 8:16, :].reshape(384, 64))
    rows_from_slab(rows, 3, padded[8:56, 48:56, :].reshape(384, 64))
    pieces_from_rows(a_send, rows)
    pl.semaphore_wait(barrier, TILES - 1 + LEVS - 1)
    spread_start(a_send, a_recv, send_sem.at[0], recv_sem.at[0], me)

    wide_view = wanted.reshape(32, 8, 3)

    def want(m, carry):
        for h in range(2):
            wide_view[m, 4 * h : 4 * h + 4, :] = seam_v[2 * m + h]
        return carry

    lax.fori_loop(0, 32, want, 0)
    table = wanted[...]
    wished = table[:, 0:1] * 4 + table[:, 1:2]
    for j in range(2):
        choice[:, 128 * j : 128 * j + 128] = jnp.where(
            wished == iota((256, 128), 1) + 128 * j, 1.0, 0.0
        ).astype(BF16)
    for side in range(4):
        turns[0, side] = turn_matrix(side, seam[me, side, 1], seam[me, side, 2], False)

    spread_wait(a_send, a_recv, send_sem.at[0], recv_sem.at[0])
    rows_from_pieces(rows, a_recv)
    pick(rows, choice[...])
    pieces_from_rows(b_send, rows)
    spread_start(b_send, b_recv, send_sem.at[1], recv_sem.at[1], me)

    for side in range(4):
        turns[1, side] = turn_matrix(side, seam[me, side, 1], seam[me, side, 2], True)

    spread_wait(b_send, b_recv, send_sem.at[1], recv_sem.at[1])
    rows_from_pieces(rows, b_recv)
    rims = [dot(turns[0, side], slab_from_rows(rows, side).astype(BF16)) for side in range(4)]
    padded[0:8, 8:56, :] = rims[0].reshape(8, 48, 64)
    padded[56:64, 8:56, :] = rims[1].reshape(8, 48, 64)
    padded[8:56, 0:8, :] = rims[2].reshape(48, 8, 64)
    padded[8:56, 56:64, :] = rims[3].reshape(48, 8, 64)

    def widen(c, carry):
        x = padded[pl.ds(8 * c, 8)]
        wide[pl.ds(8 * c, 8)] = jnp.concatenate([x[:, 0:48], x[:, 8:56], x[:, 16:64]], axis=2).astype(BF16)
        return carry

    lax.fori_loop(0, 8, widen, 0)
    down = down_ref[...]
    up = up_ref[...]
    forward = [
        jnp.concatenate([conv_w[3 * a + b] for b in range(3)], axis=1) for a in range(3)
    ]

    def conv(c, carry):
        total = jnp.zeros((384, 64), F32)
        for a in range(3):
            total += dot(wide[pl.ds(8 * (c + a), 8)].reshape(384, 192), forward[a], NT)
        second[c] = total
        s = (total * jax.nn.sigmoid(total)).astype(BF16)
        act[c] = s
        lat[level, c] = dot(down, s, NT).astype(BF16)
        return carry

    lax.fori_loop(0, 6, conv, 0)
    level_start(lat, send_sem.at[2], recv_sem.at[2], level)

    head = head_ref[...]
    high = head.astype(BF16)
    rest = head - high.astype(F32)
    middle = rest.astype(BF16)
    low = (rest - middle.astype(F32)).astype(BF16)
    zero_rows = jnp.zeros((5, 64), F32)
    heads = jnp.concatenate(
        [high.astype(F32), middle.astype(F32), low.astype(F32), zero_rows], axis=0
    ).astype(BF16)
    eye = jnp.where(iota((8, 8), 0) == iota((8, 8), 1), 1.0, 0.0).astype(BF16)
    up_t = dot(eye, up, NT).astype(BF16)

    level_wait(lat, send_sem.at[2], recv_sem.at[2])

    def top_step(c, carry):
        mixed = mix_ref[level, 0] * lat[0, c].astype(F32)
        for other in range(1, LEVS):
            mixed += mix_ref[level, other] * lat[other, c].astype(F32)
        mixed = mixed.astype(BF16).astype(F32).T.astype(BF16)
        third = act[c].astype(F32) + dot(mixed, up, NT)
        cot = jnp.broadcast_to(cot_ref[c].astype(F32), (8, 384)).T.astype(BF16)
        gradient = dot(cot, heads) * dsilu(third)
        top[c] = gradient
        glat[level, c] = dot(up_t, gradient.astype(BF16), NT).astype(BF16)
        return carry

    lax.fori_loop(0, 6, top_step, 0)
    level_start(glat, send_sem.at[3], recv_sem.at[3], level)

    def clear(c, carry):
        deep_wide[pl.ds(8 * c, 8)] = jnp.zeros((8, 64, 192), BF16)
        deep_wide[pl.ds(64 + 8 * c, 8)] = jnp.zeros((8, 64, 192), BF16)
        return carry

    lax.fori_loop(0, 2, clear, 0)
    shallow[0:8] = jnp.zeros((8, 48, 64), BF16)
    shallow[56:64] = jnp.zeros((8, 48, 64), BF16)
    level_wait(glat, send_sem.at[3], recv_sem.at[3])

    def deep_step(c, carry):
        mixed = mix_ref[0, level] * glat[0, c].astype(F32)
        for other in range(1, LEVS):
            mixed += mix_ref[other, level] * glat[other, c].astype(F32)
        mixed = mixed.astype(BF16).astype(F32).T.astype(BF16)
        gradient = top[c] + dot(mixed, down)
        d = (gradient * dsilu(second[c])).reshape(8, 48, 64)
        z8 = jnp.zeros((8, 8, 64), F32)
        z16 = jnp.zeros((8, 16, 64), F32)
        joined = jnp.concatenate(
            [
                jnp.concatenate([d, z16], axis=1),
                jnp.concatenate([z8, d, z8], axis=1),
                jnp.concatenate([z16, d], axis=1),
            ],
            axis=2,
        )
        deep_wide[pl.ds(8 * c + 16, 8)] = joined.astype(BF16)
        return carry

    lax.fori_loop(0, 6, deep_step, 0)
    backward = [conv_w[3 * a : 3 * a + 3].reshape(192, 64) for a in range(3)]

    def adjoint(c, carry):
        total = jnp.zeros((512, 64), F32)
        for a in range(3):
            total += dot(deep_wide[pl.ds(8 * (c + 2 - a), 8)].reshape(512, 192), backward[a])
        grad[pl.ds(8 * c, 8)] = total.reshape(8, 64, 64)
        return carry

    lax.fori_loop(0, 8, adjoint, 0)
    rows_from_slab(rows, 0, grad[0:8, 8:56, :].reshape(384, 64))
    rows_from_slab(rows, 1, grad[56:64, 8:56, :].reshape(384, 64))
    rows_from_slab(rows, 2, grad[8:56, 0:8, :].reshape(384, 64))
    rows_from_slab(rows, 3, grad[8:56, 56:64, :].reshape(384, 64))
    pieces_from_rows(c_send, rows)
    spread_start(c_send, c_recv, send_sem.at[4], recv_sem.at[4], me)

    def slope(c, carry):
        pre_t[pl.ds(8 * c, 8)] = dsilu(pre_t[pl.ds(8 * c, 8)])
        return carry

    lax.fori_loop(0, 6, slope, 0)
    cell = iota((8, 2304), 1)
    row = jnp.zeros((8, 2304), jnp.int32)
    for i in range(1, 48):
        row += jnp.where(cell >= 48 * i, 1, 0)
    column = cell - 48 * row
    for side in range(4):
        edge, flip = seam[me, side, 1], seam[me, side, 2]
        a, b = [(row, column), (47 - row, column), (column, row), (47 - column, row)][side]
        turned = 1 - lax.rem(edge, 2)
        by_rows = jnp.where(edge < 2, 1, 0)
        depth = turned * 3 + (1 - 2 * turned) * a
        along = flip * 47 + (1 - 2 * flip) * b
        index = depth * (1 + 47 * by_rows) + along * (4 - 3 * by_rows)
        index = jnp.where(a < 4, index, -1)

        def put(k, carry, side=side, index=index):
            base = pl.multiple_of(16 * k, 16)
            low_half = jnp.where(index == iota((8, 2304), 0) + base, 1.0, 0.0)
            high_half = jnp.where(index == iota((8, 2304), 0) + base + 8, 1.0, 0.0)
            place[pl.ds(pl.multiple_of(192 * side + base, 16), 16), :] = jnp.concatenate(
                [low_half, high_half], axis=0
            ).astype(BF16)
            return carry

        lax.fori_loop(0, 12, put, 0)

    spread_wait(c_send, c_recv, send_sem.at[4], recv_sem.at[4])
    rows_from_pieces(rows, c_recv)
    pick(rows, choice[...])
    pieces_from_rows(d_send, rows)
    spread_start(d_send, d_recv, send_sem.at[5], recv_sem.at[5], me)
    spread_wait(d_send, d_recv, send_sem.at[5], recv_sem.at[5])
    rows_from_pieces(rows, d_recv)
    rims = [dot(turns[1, side], slab_from_rows(rows, side).astype(BF16)) for side in range(4)]
    grad[8:16, 8:56, :] += rims[0].reshape(8, 48, 64)
    grad[48:56, 8:56, :] += rims[1].reshape(8, 48, 64)
    grad[8:56, 8:16, :] += rims[2].reshape(48, 8, 64)
    grad[8:56, 48:56, :] += rims[3].reshape(48, 8, 64)

    def shallow_step(c, carry):
        shallow[pl.ds(8 * c + 8, 8)] = (
            grad[pl.ds(8 * c + 8, 8), 8:56, :] * pre_t[pl.ds(8 * c, 8)]
        ).astype(BF16)
        return carry

    lax.fori_loop(0, 6, shallow_step, 0)
    blank = jnp.zeros((64, 122), F32)
    inner = [
        jnp.concatenate([in_w[3 * a + b].astype(F32) for b in range(3)] + [blank], axis=1).astype(BF16)
        for a in range(3)
    ]
    for c in range(7):
        total = jnp.zeros((384, 128), F32)
        for a in range(3):
            total += dot(shallow[8 * c + 8 - 4 * a : 8 * c + 16 - 4 * a].reshape(384, 64), inner[a])
        bands_t[:, 384 * c : 384 * c + 384] = total.T[0:8]
    taps = bands_t[...]
    centre, left, right = taps[2:4], taps[0:2], taps[4:6]
    position = iota((2, 2688), 1)
    line = jnp.zeros((2, 2688), jnp.int32)
    for i in range(1, 56):
        line += jnp.where(position >= 48 * i, 1, 0)
    at = position - 48 * line
    whole = (
        centre
        + jnp.where(at < 44, pltpu.roll(left, 2684, 1), 0.0)
        + jnp.where(at >= 4, pltpu.roll(right, 4, 1), 0.0)
    )
    inside = taps[:, 192:2496].astype(BF16).astype(F32)
    stacked = jnp.concatenate([inside[:, 384 * c : 384 * c + 384] for c in range(6)], axis=0)
    lane, cell8 = iota((384, 128), 1), iota((384, 128), 0)
    half = lane // 32
    source = ((lane % 32) // 4) * 48 + lane % 4 + 44 * half
    taken = jnp.where((source == cell8) & (lane < 64), 1.0, 0.0).astype(BF16)
    sides = dot(stacked.astype(BF16), taken)
    message = [
        jnp.concatenate([whole[0:1, 0:192], whole[1:2, 0:192]], axis=1),
        jnp.concatenate([whole[0:1, 2496:2688], whole[1:2, 2496:2688]], axis=1),
        jnp.concatenate([sides[8 * c + j : 8 * c + j + 1, 0:32] for j in range(2) for c in range(6)], axis=1),
        jnp.concatenate([sides[8 * c + 4 + j : 8 * c + 5 + j, 32:64] for j in range(2) for c in range(6)], axis=1),
    ]
    message = jnp.concatenate(message, axis=0)
    for j in range(3):
        e_send[j] = message[:, 128 * j : 128 * j + 128].astype(BF16)
        e_recv[me, j] = message[:, 128 * j : 128 * j + 128].astype(BF16)

    def tell(i, carry):
        pltpu.make_async_remote_copy(
            e_send, e_recv.at[me], send_sem.at[6], recv_sem.at[6],
            device_id={"tile": lax.rem(me + i, TILES)}, device_id_type=MESH,
        ).start()
        return carry

    lax.fori_loop(1, TILES, tell, 0)
    own = jnp.zeros((8, 256), jnp.int32) - 1
    for side in range(4):
        own = jnp.where(iota((8, 256), 0) == side, seam[me, side, 0] * 4 + seam[me, side, 1], own)
    chosen = jnp.where(own == iota((8, 256), 1), 1.0, 0.0).astype(BF16)
    active = jnp.where(panel[me] < 6, 1.0, 0.0)
    others = pl.ds(0, TILES - 1)
    pltpu.make_async_copy(e_recv.at[others], e_recv.at[others], recv_sem.at[6]).wait()
    pltpu.make_async_copy(e_recv.at[others], e_recv.at[others], send_sem.at[6]).wait()
    rows_from_pieces(rows, e_recv)
    came = jnp.concatenate([dot(chosen, rows[j].astype(BF16)) for j in range(3)], axis=1)
    arrived = jnp.concatenate(
        [
            jnp.concatenate([came[i : i + 1, 192 * j : 192 * j + 192] for i in range(4)], axis=1)
            for j in range(2)
        ]
        + [jnp.zeros((6, 768), F32)],
        axis=0,
    )
    added = dot(arrived.astype(BF16), place[...])
    out_ref[0, 0] = (whole[:, 192:2496] + added[0:2]) * active


def shards(
    pre_act, cotangent, input_weight, conv_weight, down_weight, level_mix, up_weight, head_weight, seam_list,
    tile_panel,
):
    vmem = pl.BlockSpec(memory_space=pltpu.VMEM)
    smem = pl.BlockSpec(memory_space=pltpu.SMEM)
    pieces = pltpu.VMEM((TILES, 3, 4, 128), BF16)
    return pl.pallas_call(
        kernel,
        out_shape=jax.ShapeDtypeStruct((1, 1, 2, 2304), F32),
        in_specs=[vmem, vmem, vmem, vmem, vmem, smem, vmem, vmem, smem, vmem, smem],
        out_specs=vmem,
        scratch_shapes=[
            pltpu.VMEM((48, 48, 64), F32),
            pltpu.VMEM((64, 64, 64), F32),
            pltpu.VMEM((64, 48, 192), BF16),
            pltpu.VMEM((6, 384, 64), BF16),
            pltpu.VMEM((6, 384, 64), F32),
            pltpu.VMEM((6, 384, 64), F32),
            pltpu.VMEM((80, 64, 192), BF16),
            pltpu.VMEM((64, 64, 64), F32),
            pltpu.VMEM((64, 48, 64), BF16),
            pltpu.VMEM((8, 2688), F32),
            pltpu.VMEM((2, 4, 384, 384), BF16),
            pltpu.VMEM((768, 2304), BF16),
            pltpu.VMEM((3, 256, 128), F32),
            pltpu.VMEM((256, 3), jnp.int32),
            pltpu.VMEM((256, 256), BF16),
        ]
        + [pieces] * 8
        + [
            pltpu.VMEM((3, 4, 128), BF16),
            pieces,
            pltpu.VMEM((LEVS, 6, 8, 384), BF16),
            pltpu.VMEM((LEVS, 6, 8, 384), BF16),
            pltpu.SemaphoreType.DMA((7,)),
            pltpu.SemaphoreType.DMA((7,)),
        ],
        compiler_params=pltpu.CompilerParams(
            collective_id=0, has_side_effects=True, vmem_limit_bytes=48 * 2**20
        ),
        name="adjoint",
    )(
        pre_act, cotangent.reshape(6, 1, 384), input_weight, conv_weight, down_weight, level_mix, up_weight,
        head_weight.reshape(1, 64), seam_list, seam_list, tile_panel,
    )


def solution(mesh):
    return jax.shard_map(
        shards,
        mesh=mesh,
        in_specs=(P("tile", "lev", None, None), P("tile", "lev", None), P(), P(), P(), P(), P(), P(), P(), P()),
        out_specs=P("tile", "lev", None, None),
        check_vma=False,
    )
```

```python
import functools

import jax
import jax.numpy as jnp
from jax import lax
from jax.experimental import pallas as pl
from jax.experimental.pallas import tpu as pltpu
from jax.sharding import PartitionSpec as P

F32 = jnp.float32
BF16 = jnp.bfloat16
MESH = pl.DeviceIdType.MESH
NT = (((1,), (1,)), ((), ()))
NN = (((1,), (0,)), ((), ()))
TILES = 64
LEVS = 8


def dot(a, b, dims=NN):
    return lax.dot_general(a, b, dims, preferred_element_type=F32)


def dsilu(v):
    g = jax.nn.sigmoid(v)
    return g * (1.0 + v * (1.0 - g))


def iota(shape, axis):
    return lax.broadcasted_iota(jnp.int32, shape, axis)


def peer_at(me, i):
    back = TILES - i
    half = (back + 1) // 2
    return jnp.bitwise_and(me + jnp.where(lax.rem(back, 2) == 1, half, TILES - half), TILES - 1)


def rows_from_pieces(rows, j, pieces):
    view = rows.reshape(3, 32, 8, 128)

    def step(m, carry):
        for k in range(4):
            for h in range(2):
                view[j, 4 * m + k, 4 * h : 4 * h + 4, :] = pieces[8 * m + 2 * k + h].astype(F32)
        return carry

    lax.fori_loop(0, 8, step, 0)


def pieces_from_rows(pieces, rows, j):
    view = rows.reshape(3, 32, 8, 128)

    def step(m, carry):
        for k in range(4):
            for h in range(2):
                pieces[8 * m + 2 * k + h] = view[j, 4 * m + k, 4 * h : 4 * h + 4, :].astype(BF16)
        return carry

    lax.fori_loop(0, 8, step, 0)


def slab_to_rows(rows, j, member, slab):
    rows[j, pl.ds(member, 64, stride=4), :] = jnp.concatenate([slab[0:64], slab[64:128]], axis=1)


def slab_from_rows(rows, member):
    parts = []
    for j in range(3):
        block = rows[j, pl.ds(member, 64, stride=4), :]
        parts += [block[:, :64], block[:, 64:]]
    return jnp.concatenate(parts, axis=0)


def spread_start(send, recv, sems, me):
    recv[me] = send[me]

    def step(i, carry):
        target = peer_at(me, i)
        pltpu.make_async_remote_copy(
            send.at[target], recv.at[me], sems.at[0], sems.at[1],
            device_id={"tile": target}, device_id_type=MESH,
        ).start()
        return carry

    lax.fori_loop(1, TILES, step, 0)


def arrived_all(ref, count, sem):
    some = ref.at[pl.ds(0, count)]
    pltpu.make_async_copy(some, some, sem).wait()


def strips_out(slabs, rows, send, recv, sems, me):
    for j in range(3):
        for member in range(4):
            slab_to_rows(rows, j, member, slabs[member](j))
        pieces_from_rows(send.at[j], rows, j)
        spread_start(send.at[j], recv.at[j], sems.at[j], me)


def strips_on(choice, rows, first_recv, first_sems, send, recv, sems, me):
    for j in range(3):
        arrived_all(first_recv.at[j], TILES - 1, first_sems.at[j, 1])
        rows_from_pieces(rows, j, first_recv.at[j])
        rows[j] = dot(choice[...], rows[j].astype(BF16))
        pieces_from_rows(send.at[j], rows, j)
        spread_start(send.at[j], recv.at[j], sems.at[j], me)


def strips_in(turns, rows, recv, sems):
    for j in range(3):
        arrived_all(recv.at[j], TILES - 1, sems.at[j, 1])
        rows_from_pieces(rows, j, recv.at[j])
    return [dot(turns[side], slab_from_rows(rows, side).astype(BF16)) for side in range(4)]


def level_start(buf, c, sems, level):
    for i in (4, 3, 5, 2, 6, 1, 7):
        pltpu.make_async_remote_copy(
            buf.at[c, level], buf.at[c, level], sems.at[c, 0], sems.at[c, 1],
            device_id={"lev": jnp.bitwise_and(level + i, LEVS - 1)}, device_id_type=MESH,
        ).start()


def turn_matrix(side, edge, flip, of_bands):
    if side < 2:
        r, b = iota((8, 48, 128), 0), iota((8, 48, 128), 1)
    else:
        b, r = iota((48, 8, 128), 0), iota((48, 8, 128), 1)
    r, b = r.reshape(384, 128), b.reshape(384, 128)
    turned_here = (side % 2 == 0) if not of_bands else (side % 2 == 1)
    a = 7 - r if turned_here else r
    odd = lax.rem(edge, 2)
    turned_there = odd if not of_bands else 1 - odd
    depth = turned_there * 7 + (1 - 2 * turned_there) * a
    along = flip * 47 + (1 - 2 * flip) * b
    by_rows = jnp.where(edge < 2, 1, 0)
    index = depth * (1 + 47 * by_rows) + along * (8 - 7 * by_rows)
    lanes = iota((384, 128), 1)
    return jnp.concatenate(
        [jnp.where(index == lanes + 128 * j, 1.0, 0.0).astype(BF16) for j in range(3)], axis=1
    )


def kernel(
    pre_ref, cot_ref, in_w, conv_w, down_ref, mix_ref, up_ref, head_ref, seam, seam_v, panel, out_ref,
    pre_t, padded, wide, act, second, top, deep_wide, grad, shallow, bands_t, turns, place, rows, wanted,
    choice, a_send, a_recv, b_send, b_recv, c_send, c_recv, d_send, d_recv, e_send, e_recv, f_send, f_recv, lat, glat,
    tile_sems, lat_sems, glat_sems, last_sems,
):
    me = lax.axis_index("tile")
    level = lax.axis_index("lev")
    barrier = pltpu.get_barrier_semaphore()

    def greet(i, carry):
        pl.semaphore_signal(barrier, inc=1, device_id={"tile": peer_at(me, i)}, device_id_type=MESH)
        return carry

    lax.fori_loop(1, TILES, greet, 0)
    for i in range(1, LEVS):
        pl.semaphore_signal(barrier, inc=1, device_id={"lev": lax.rem(level + i, LEVS)}, device_id_type=MESH)

    pre_t[...] = pre_ref[0, 0].astype(F32).T.reshape(48, 48, 64)
    padded[0:8] = jnp.zeros((8, 64, 64), F32)
    padded[56:64] = jnp.zeros((8, 64, 64), F32)

    def first(c, carry):
        v = pre_t[pl.ds(8 * c, 8)]
        s = v * jax.nn.sigmoid(v)
        padded[pl.ds(8 * c + 8, 8), 8:56, :] = s.astype(BF16).astype(F32)
        return carry

    lax.fori_loop(0, 6, first, 0)
    pl.semaphore_wait(barrier, TILES - 1 + LEVS - 1)

    def edges_of(ref, places):
        def rows_at(r, c0):
            return lambda j: ref[r : r + 8, c0 : c0 + 48, :].reshape(384, 64)[128 * j : 128 * j + 128]

        def columns_at(r, c0):
            return lambda j: ref[r + 16 * j : r + 16 * j + 16, c0 : c0 + 8, :].reshape(128, 64)

        return [rows_at(*places[0]), rows_at(*places[1]), columns_at(*places[2]), columns_at(*places[3])]

    strips_out(
        edges_of(padded, [(8, 8), (48, 8), (8, 8), (8, 48)]), rows, a_send, a_recv, tile_sems.at[0], me
    )

    wide_view = wanted.reshape(32, 8, 3)

    def want(m, carry):
        for h in range(2):
            wide_view[m, 4 * h : 4 * h + 4, :] = seam_v[2 * m + h]
        return carry

    lax.fori_loop(0, 32, want, 0)
    table = wanted[...]
    wished = table[:, 0:1] * 4 + table[:, 1:2]
    for j in range(2):
        choice[:, 128 * j : 128 * j + 128] = jnp.where(
            wished == iota((256, 128), 1) + 128 * j, 1.0, 0.0
        ).astype(BF16)
    for side in range(4):
        turns[0, side] = turn_matrix(side, seam[me, side, 1], seam[me, side, 2], False)

    strips_on(choice, rows, a_recv, tile_sems.at[0], b_send, b_recv, tile_sems.at[1], me)

    for side in range(4):
        turns[1, side] = turn_matrix(side, seam[me, side, 1], seam[me, side, 2], True)

    rims = strips_in(turns.at[0], rows, b_recv, tile_sems.at[1])
    padded[0:8, 8:56, :] = rims[0].reshape(8, 48, 64)
    padded[56:64, 8:56, :] = rims[1].reshape(8, 48, 64)
    padded[8:56, 0:8, :] = rims[2].reshape(48, 8, 64)
    padded[8:56, 56:64, :] = rims[3].reshape(48, 8, 64)

    def widen(c, carry):
        x = padded[pl.ds(8 * c, 8)]
        wide[pl.ds(8 * c, 8)] = jnp.concatenate([x[:, 0:48], x[:, 8:56], x[:, 16:64]], axis=2).astype(BF16)
        return carry

    lax.fori_loop(0, 8, widen, 0)
    down = down_ref[...]
    up = up_ref[...]
    forward = [
        jnp.concatenate([conv_w[3 * a + b] for b in range(3)], axis=1) for a in range(3)
    ]

    def conv(c, carry):
        total = jnp.zeros((384, 64), F32)
        for a in range(3):
            total += dot(wide[pl.ds(8 * (c + a), 8)].reshape(384, 192), forward[a], NT)
        second[c] = total
        s = (total * jax.nn.sigmoid(total)).astype(BF16)
        act[c] = s
        lat[c, level] = dot(down, s, NT).astype(BF16)
        level_start(lat, c, lat_sems, level)
        return carry

    lax.fori_loop(0, 6, conv, 0)

    head = head_ref[...]
    high = head.astype(BF16)
    rest = head - high.astype(F32)
    middle = rest.astype(BF16)
    low = (rest - middle.astype(F32)).astype(BF16)
    zero_rows = jnp.zeros((5, 64), F32)
    heads = jnp.concatenate(
        [high.astype(F32), middle.astype(F32), low.astype(F32), zero_rows], axis=0
    ).astype(BF16)
    eye = jnp.where(iota((8, 8), 0) == iota((8, 8), 1), 1.0, 0.0).astype(BF16)
    up_t = dot(eye, up, NT).astype(BF16)

    def clear(c, carry):
        deep_wide[pl.ds(8 * c, 8)] = jnp.zeros((8, 64, 192), BF16)
        deep_wide[pl.ds(64 + 8 * c, 8)] = jnp.zeros((8, 64, 192), BF16)
        return carry

    lax.fori_loop(0, 2, clear, 0)
    shallow[0:8] = jnp.zeros((8, 48, 64), BF16)
    shallow[56:64] = jnp.zeros((8, 48, 64), BF16)

    def top_step(c, carry):
        arrived_all(lat.at[c], LEVS - 1, lat_sems.at[c, 1])
        mixed = mix_ref[level, 0] * lat[c, 0].astype(F32)
        for other in range(1, LEVS):
            mixed += mix_ref[level, other] * lat[c, other].astype(F32)
        mixed = mixed.astype(BF16).astype(F32).T.astype(BF16)
        third = act[c].astype(F32) + dot(mixed, up, NT)
        cot = jnp.broadcast_to(cot_ref[c].astype(F32), (8, 384)).T.astype(BF16)
        gradient = dot(cot, heads) * dsilu(third)
        top[c] = gradient
        glat[c, level] = dot(up_t, gradient.astype(BF16), NT).astype(BF16)
        level_start(glat, c, glat_sems, level)
        return carry


    lax.fori_loop(0, 6, top_step, 0)

    def deep_step(c, carry):
        arrived_all(glat.at[c], LEVS - 1, glat_sems.at[c, 1])
        mixed = mix_ref[0, level] * glat[c, 0].astype(F32)
        for other in range(1, LEVS):
            mixed += mix_ref[other, level] * glat[c, other].astype(F32)
        mixed = mixed.astype(BF16).astype(F32).T.astype(BF16)
        gradient = top[c] + dot(mixed, down)
        d = (gradient * dsilu(second[c])).reshape(8, 48, 64)
        z8 = jnp.zeros((8, 8, 64), F32)
        z16 = jnp.zeros((8, 16, 64), F32)
        joined = jnp.concatenate(
            [
                jnp.concatenate([d, z16], axis=1),
                jnp.concatenate([z8, d, z8], axis=1),
                jnp.concatenate([z16, d], axis=1),
            ],
            axis=2,
        )
        deep_wide[pl.ds(8 * c + 16, 8)] = joined.astype(BF16)
        return carry

    lax.fori_loop(0, 6, deep_step, 0)
    backward = [conv_w[3 * a : 3 * a + 3].reshape(192, 64) for a in range(3)]

    def adjoint(c, carry):
        total = jnp.zeros((512, 64), F32)
        for a in range(3):
            total += dot(deep_wide[pl.ds(8 * (c + 2 - a), 8)].reshape(512, 192), backward[a])
        grad[pl.ds(8 * c, 8)] = total.reshape(8, 64, 64)
        return carry

    lax.fori_loop(0, 8, adjoint, 0)
    strips_out(
        edges_of(grad, [(0, 8), (56, 8), (8, 0), (8, 56)]), rows, c_send, c_recv, tile_sems.at[2], me
    )

    def slope(c, carry):
        pre_t[pl.ds(8 * c, 8)] = dsilu(pre_t[pl.ds(8 * c, 8)])
        return carry

    lax.fori_loop(0, 6, slope, 0)
    cell = iota((8, 2304), 1)
    row = jnp.zeros((8, 2304), jnp.int32)
    for i in range(1, 48):
        row += jnp.where(cell >= 48 * i, 1, 0)
    column = cell - 48 * row
    for side in range(4):
        edge, flip = seam[me, side, 1], seam[me, side, 2]
        a, b = [(row, column), (47 - row, column), (column, row), (47 - column, row)][side]
        turned = 1 - lax.rem(edge, 2)
        by_rows = jnp.where(edge < 2, 1, 0)
        depth = turned * 3 + (1 - 2 * turned) * a
        along = flip * 47 + (1 - 2 * flip) * b
        index = depth * (1 + 47 * by_rows) + along * (4 - 3 * by_rows)
        index = jnp.where(a < 4, index, -1)

        def put(k, carry, side=side, index=index):
            base = pl.multiple_of(16 * k, 16)
            low_half = jnp.where(index == iota((8, 2304), 0) + base, 1.0, 0.0)
            high_half = jnp.where(index == iota((8, 2304), 0) + base + 8, 1.0, 0.0)
            place[pl.ds(pl.multiple_of(192 * side + base, 16), 16), :] = jnp.concatenate(
                [low_half, high_half], axis=0
            ).astype(BF16)
            return carry

        lax.fori_loop(0, 12, put, 0)

    strips_on(choice, rows, c_recv, tile_sems.at[2], d_send, d_recv, tile_sems.at[3], me)
    rims = strips_in(turns.at[1], rows, d_recv, tile_sems.at[3])
    grad[8:16, 8:56, :] += rims[0].reshape(8, 48, 64)
    grad[48:56, 8:56, :] += rims[1].reshape(8, 48, 64)
    grad[8:56, 8:16, :] += rims[2].reshape(48, 8, 64)
    grad[8:56, 48:56, :] += rims[3].reshape(48, 8, 64)

    def shallow_step(c, carry):
        shallow[pl.ds(8 * c + 8, 8)] = (
            grad[pl.ds(8 * c + 8, 8), 8:56, :] * pre_t[pl.ds(8 * c, 8)]
        ).astype(BF16)
        return carry

    lax.fori_loop(0, 6, shallow_step, 0)
    blank = jnp.zeros((64, 122), F32)
    inner = [
        jnp.concatenate([in_w[3 * a + b].astype(F32) for b in range(3)] + [blank], axis=1).astype(BF16)
        for a in range(3)
    ]
    for c in range(7):
        total = jnp.zeros((384, 128), F32)
        for a in range(3):
            total += dot(shallow[8 * c + 8 - 4 * a : 8 * c + 16 - 4 * a].reshape(384, 64), inner[a])
        bands_t[:, 384 * c : 384 * c + 384] = total.T[0:8]
    taps = bands_t[...]
    centre, left, right = taps[2:4], taps[0:2], taps[4:6]
    position = iota((2, 2688), 1)
    line = jnp.zeros((2, 2688), jnp.int32)
    for i in range(1, 56):
        line += jnp.where(position >= 48 * i, 1, 0)
    at = position - 48 * line
    whole = (
        centre
        + jnp.where(at < 44, pltpu.roll(left, 2684, 1), 0.0)
        + jnp.where(at >= 4, pltpu.roll(right, 4, 1), 0.0)
    )
    inside = taps[:, 192:2496].astype(BF16).astype(F32)
    stacked = jnp.concatenate([inside[:, 384 * c : 384 * c + 384] for c in range(6)], axis=0)
    lane, cell8 = iota((384, 128), 1), iota((384, 128), 0)
    half = lane // 32
    source = ((lane % 32) // 4) * 48 + lane % 4 + 44 * half
    taken = jnp.where((source == cell8) & (lane < 64), 1.0, 0.0).astype(BF16)
    sides = dot(stacked.astype(BF16), taken)
    message = [
        jnp.concatenate([whole[0:1, 0:192], whole[1:2, 0:192]], axis=1),
        jnp.concatenate([whole[0:1, 2496:2688], whole[1:2, 2496:2688]], axis=1),
        jnp.concatenate([sides[8 * c + j : 8 * c + j + 1, 0:32] for j in range(2) for c in range(6)], axis=1),
        jnp.concatenate([sides[8 * c + 4 + j : 8 * c + 5 + j, 32:64] for j in range(2) for c in range(6)], axis=1),
    ]
    message = jnp.concatenate(message, axis=0)
    depth, quarter = me // 4, lax.rem(me, 4)
    for j in range(3):
        e_send[j] = message[:, 128 * j : 128 * j + 128].astype(BF16)
        e_recv[depth, j] = message[:, 128 * j : 128 * j + 128].astype(BF16)

    def tell(i, carry):
        back = 16 - i
        half = (back + 1) // 2
        there = jnp.bitwise_and(depth + jnp.where(lax.rem(back, 2) == 1, half, 16 - half), 15)
        pltpu.make_async_remote_copy(
            e_send, e_recv.at[depth], last_sems.at[0, 0], last_sems.at[0, 1],
            device_id={"tile": 4 * there + quarter}, device_id_type=MESH,
        ).start()
        return carry

    lax.fori_loop(1, 16, tell, 0)
    row_of = iota((16, 64), 0)
    own = jnp.zeros((16, 64), jnp.int32) - 1
    for member in range(4):
        for side in range(4):
            peer = seam[4 * depth + member, side, 0]
            held = jnp.where(lax.rem(peer, 4) == quarter, (peer // 4) * 4 + seam[4 * depth + member, side, 1], -1)
            own = jnp.where(row_of == 4 * member + side, held, own)
    chosen = jnp.where(own == iota((16, 64), 1), 1.0, 0.0).astype(BF16)
    active = jnp.where(panel[me] < 6, 1.0, 0.0)
    arrived_all(e_recv, 15, last_sems.at[0, 1])
    for j in range(3):
        view = rows.reshape(3, 32, 8, 128)
        for m in range(8):
            for h in range(2):
                view[j, m, 4 * h : 4 * h + 4, :] = e_recv[2 * m + h, j].astype(F32)
        found = dot(chosen, rows[j, 0:64].astype(BF16))
        for member in range(4):
            f_send[member, j] = found[4 * member : 4 * member + 4].astype(BF16)
    f_recv[quarter] = f_send[quarter]
    for i in (3, 2, 1):
        there = jnp.bitwise_xor(quarter, i)
        pltpu.make_async_remote_copy(
            f_send.at[there], f_recv.at[quarter], last_sems.at[1, 0], last_sems.at[1, 1],
            device_id={"tile": 4 * depth + there}, device_id_type=MESH,
        ).start()
    arrived_all(f_recv, 3, last_sems.at[1, 1])
    came = []
    for j in range(3):
        part = f_recv[0, j].astype(F32)
        for member in range(1, 4):
            part += f_recv[member, j].astype(F32)
        came.append(part)
    came = jnp.concatenate(came, axis=1)
    arrived = jnp.concatenate(
        [
            jnp.concatenate([came[i : i + 1, 192 * j : 192 * j + 192] for i in range(4)], axis=1)
            for j in range(2)
        ]
        + [jnp.zeros((6, 768), F32)],
        axis=0,
    )
    added = dot(arrived.astype(BF16), place[...])
    out_ref[0, 0] = (whole[:, 192:2496] + added[0:2]) * active
    for phase, buf in enumerate((a_send, b_send, c_send, d_send)):
        for j in range(3):
            arrived_all(buf.at[j], TILES - 1, tile_sems.at[phase, j, 0])
    for c in range(6):
        arrived_all(lat.at[c], LEVS - 1, lat_sems.at[c, 0])
        arrived_all(glat.at[c], LEVS - 1, glat_sems.at[c, 0])
    arrived_all(e_recv, 15, last_sems.at[0, 0])
    arrived_all(f_send, 3, last_sems.at[1, 0])


def shards(
    pre_act, cotangent, input_weight, conv_weight, down_weight, level_mix, up_weight, head_weight, seam_list,
    tile_panel,
):
    vmem = pl.BlockSpec(memory_space=pltpu.VMEM)
    smem = pl.BlockSpec(memory_space=pltpu.SMEM)
    pieces = pltpu.VMEM((3, TILES, 4, 128), BF16)
    return pl.pallas_call(
        kernel,
        out_shape=jax.ShapeDtypeStruct((1, 1, 2, 2304), F32),
        in_specs=[vmem, vmem, vmem, vmem, vmem, smem, vmem, vmem, smem, vmem, smem],
        out_specs=vmem,
        scratch_shapes=[
            pltpu.VMEM((48, 48, 64), F32),
            pltpu.VMEM((64, 64, 64), F32),
            pltpu.VMEM((64, 48, 192), BF16),
            pltpu.VMEM((6, 384, 64), BF16),
            pltpu.VMEM((6, 384, 64), F32),
            pltpu.VMEM((6, 384, 64), F32),
            pltpu.VMEM((80, 64, 192), BF16),
            pltpu.VMEM((64, 64, 64), F32),
            pltpu.VMEM((64, 48, 64), BF16),
            pltpu.VMEM((8, 2688), F32),
            pltpu.VMEM((2, 4, 384, 384), BF16),
            pltpu.VMEM((768, 2304), BF16),
            pltpu.VMEM((3, 256, 128), F32),
            pltpu.VMEM((256, 3), jnp.int32),
            pltpu.VMEM((256, 256), BF16),
        ]
        + [pieces] * 8
        + [
            pltpu.VMEM((3, 4, 128), BF16),
            pltpu.VMEM((16, 3, 4, 128), BF16),
            pltpu.VMEM((4, 3, 4, 128), BF16),
            pltpu.VMEM((4, 3, 4, 128), BF16),
            pltpu.VMEM((6, LEVS, 8, 384), BF16),
            pltpu.VMEM((6, LEVS, 8, 384), BF16),
            pltpu.SemaphoreType.DMA((4, 3, 2)),
            pltpu.SemaphoreType.DMA((6, 2)),
            pltpu.SemaphoreType.DMA((6, 2)),
            pltpu.SemaphoreType.DMA((2, 2)),
        ],
        compiler_params=pltpu.CompilerParams(
            collective_id=0, has_side_effects=True, vmem_limit_bytes=48 * 2**20
        ),
        name="adjoint",
    )(
        pre_act, cotangent.reshape(6, 1, 384), input_weight, conv_weight, down_weight, level_mix, up_weight,
        head_weight.reshape(1, 64), seam_list, seam_list, tile_panel,
    )


def solution(mesh):
    return jax.shard_map(
        shards,
        mesh=mesh,
        in_specs=(P("tile", "lev", None, None), P("tile", "lev", None), P(), P(), P(), P(), P(), P(), P(), P()),
        out_specs=P("tile", "lev", None, None),
        check_vma=False,
    )
```

```python
import functools

import jax
import jax.numpy as jnp
from jax import lax
from jax.experimental import pallas as pl
from jax.experimental.pallas import tpu as pltpu
from jax.sharding import PartitionSpec as P

F32 = jnp.float32
BF16 = jnp.bfloat16
MESH = pl.DeviceIdType.MESH
NT = (((1,), (1,)), ((), ()))
NN = (((1,), (0,)), ((), ()))
TILES = 64
LEVS = 8


def dot(a, b, dims=NN):
    return lax.dot_general(a, b, dims, preferred_element_type=F32)


def dsilu(v):
    g = jax.nn.sigmoid(v)
    return g * (1.0 + v * (1.0 - g))


def iota(shape, axis):
    return lax.broadcasted_iota(jnp.int32, shape, axis)


def peer_at(me, i):
    back = TILES - i
    half = (back + 1) // 2
    return jnp.bitwise_and(me + jnp.where(lax.rem(back, 2) == 1, half, TILES - half), TILES - 1)


def rows_from_pieces(rows, j, pieces):
    view = rows.reshape(3, 32, 8, 128)

    def step(m, carry):
        for k in range(4):
            for h in range(2):
                view[j, 4 * m + k, 4 * h : 4 * h + 4, :] = pieces[8 * m + 2 * k + h].astype(F32)
        return carry

    lax.fori_loop(0, 8, step, 0)


def pieces_from_rows(pieces, rows, j):
    view = rows.reshape(3, 32, 8, 128)

    def step(m, carry):
        for k in range(4):
            for h in range(2):
                pieces[8 * m + 2 * k + h] = view[j, 4 * m + k, 4 * h : 4 * h + 4, :].astype(BF16)
        return carry

    lax.fori_loop(0, 8, step, 0)


def slab_to_rows(rows, j, member, slab):
    rows[j, pl.ds(member, 64, stride=4), :] = jnp.concatenate([slab[0:64], slab[64:128]], axis=1)


def slab_from_rows(rows, member):
    parts = []
    for j in range(3):
        block = rows[j, pl.ds(member, 64, stride=4), :]
        parts += [block[:, :64], block[:, 64:]]
    return jnp.concatenate(parts, axis=0)


def spread_start(send, recv, sems, me):
    recv[me] = send[me]

    def step(i, carry):
        target = peer_at(me, i)
        pltpu.make_async_remote_copy(
            send.at[target], recv.at[me], sems.at[0], sems.at[1],
            device_id={"tile": target}, device_id_type=MESH,
        ).start()
        return carry

    lax.fori_loop(1, TILES, step, 0)


def arrived_all(ref, count, sem):
    some = ref.at[pl.ds(0, count)]
    pltpu.make_async_copy(some, some, sem).wait()


def strips_out(slabs, rows, send, recv, sems, me):
    for j in range(3):
        for member in range(4):
            slab_to_rows(rows, j, member, slabs[member](j))
        pieces_from_rows(send.at[j], rows, j)
        spread_start(send.at[j], recv.at[j], sems.at[j], me)


def strips_on(choice, rows, first_recv, first_sems, send, recv, sems, me):
    for j in range(3):
        arrived_all(first_recv.at[j], TILES - 1, first_sems.at[j, 1])
        rows_from_pieces(rows, j, first_recv.at[j])
        rows[j] = dot(choice[...], rows[j].astype(BF16))
        pieces_from_rows(send.at[j], rows, j)
        spread_start(send.at[j], recv.at[j], sems.at[j], me)


def strips_in(turns, rows, recv, sems):
    for j in range(3):
        arrived_all(recv.at[j], TILES - 1, sems.at[j, 1])
        rows_from_pieces(rows, j, recv.at[j])
    return [dot(turns[side], slab_from_rows(rows, side).astype(BF16)) for side in range(4)]


def level_start(buf, c, sems, level):
    for i in (4, 3, 5, 2, 6, 1, 7):
        pltpu.make_async_remote_copy(
            buf.at[c, level], buf.at[c, level], sems.at[c, 0], sems.at[c, 1],
            device_id={"lev": jnp.bitwise_and(level + i, LEVS - 1)}, device_id_type=MESH,
        ).start()


def turn_matrix(side, edge, flip, of_bands):
    if side < 2:
        r, b = iota((8, 48, 128), 0), iota((8, 48, 128), 1)
    else:
        b, r = iota((48, 8, 128), 0), iota((48, 8, 128), 1)
    r, b = r.reshape(384, 128), b.reshape(384, 128)
    turned_here = (side % 2 == 0) if not of_bands else (side % 2 == 1)
    a = 7 - r if turned_here else r
    odd = lax.rem(edge, 2)
    turned_there = odd if not of_bands else 1 - odd
    depth = turned_there * 7 + (1 - 2 * turned_there) * a
    along = flip * 47 + (1 - 2 * flip) * b
    by_rows = jnp.where(edge < 2, 1, 0)
    index = depth * (1 + 47 * by_rows) + along * (8 - 7 * by_rows)
    lanes = iota((384, 128), 1)
    return jnp.concatenate(
        [jnp.where(index == lanes + 128 * j, 1.0, 0.0).astype(BF16) for j in range(3)], axis=1
    )


def kernel(
    pre_hbm, cot_ref, in_w, conv_hbm, down_ref, mix_ref, up_ref, head_ref, seam, seam_v, panel, out_ref,
    pre_t, padded, wide, act, second, top, deep_wide, grad, shallow, bands_t, turns, place, rows, wanted,
    choice, a_send, a_recv, b_send, b_recv, c_send, c_recv, d_send, d_recv, e_send, e_recv, f_send, f_recv, lat, glat,
    tile_sems, lat_sems, glat_sems, last_sems, pre_ref, conv_w, load_sems,
):
    me = lax.axis_index("tile")
    level = lax.axis_index("lev")
    load_pre = pltpu.make_async_copy(pre_hbm, pre_ref, load_sems.at[0])
    load_pre.start()
    load_conv = pltpu.make_async_copy(conv_hbm, conv_w, load_sems.at[1])
    load_conv.start()
    barrier = pltpu.get_barrier_semaphore()

    def greet(i, carry):
        pl.semaphore_signal(barrier, inc=1, device_id={"tile": peer_at(me, i)}, device_id_type=MESH)
        return carry

    lax.fori_loop(1, TILES, greet, 0)
    for i in range(1, LEVS):
        pl.semaphore_signal(barrier, inc=1, device_id={"lev": lax.rem(level + i, LEVS)}, device_id_type=MESH)

    load_pre.wait()
    pre_t[...] = pre_ref[0, 0].astype(F32).T.reshape(48, 48, 64)
    padded[8:56, 0:8, :] = jnp.zeros((48, 8, 64), F32)
    padded[8:56, 56:64, :] = jnp.zeros((48, 8, 64), F32)

    def first(c, carry):
        v = pre_t[pl.ds(8 * c, 8)]
        s = v * jax.nn.sigmoid(v)
        padded[pl.ds(8 * c + 8, 8), 8:56, :] = s.astype(BF16).astype(F32)
        return carry

    lax.fori_loop(0, 6, first, 0)
    pl.semaphore_wait(barrier, TILES - 1 + LEVS - 1)

    def edges_of(ref, places):
        def rows_at(r, c0):
            return lambda j: ref[r : r + 8, c0 : c0 + 48, :].reshape(384, 64)[128 * j : 128 * j + 128]

        def columns_at(r, c0):
            return lambda j: ref[r + 16 * j : r + 16 * j + 16, c0 : c0 + 8, :].reshape(128, 64)

        return [rows_at(*places[0]), rows_at(*places[1]), columns_at(*places[2]), columns_at(*places[3])]

    strips_out(
        edges_of(padded, [(8, 8), (48, 8), (8, 8), (8, 48)]), rows, a_send, a_recv, tile_sems.at[0], me
    )

    wished = (seam_v[0] * 4 + seam_v[1]).astype(F32)
    wished = jnp.concatenate([wished, jnp.zeros((4, 64), F32)], axis=0)
    wished = jnp.concatenate([wished, jnp.zeros((8, 64), F32)], axis=1).T
    for side in range(4):
        wanted[pl.ds(side, 64, stride=4), :] = jnp.broadcast_to(
            wished[0:64, side : side + 1], (64, 128)
        ).astype(jnp.int32)
    table = wanted[...]
    for j in range(2):
        choice[:, 128 * j : 128 * j + 128] = jnp.where(
            table == iota((256, 128), 1) + 128 * j, 1.0, 0.0
        ).astype(BF16)

    load_conv.wait()
    wide[0:8] = jnp.zeros((8, 48, 192), BF16)
    wide[56:64] = jnp.zeros((8, 48, 192), BF16)

    def widen(c, carry):
        x = padded[pl.ds(8 * c, 8)]
        wide[pl.ds(8 * c, 8)] = jnp.concatenate([x[:, 0:48], x[:, 8:56], x[:, 16:64]], axis=2).astype(BF16)
        return carry

    lax.fori_loop(1, 7, widen, 0)
    down = down_ref[...]
    up_t = up_ref[...]
    forward = [
        jnp.concatenate([conv_w[3 * a + b] for b in range(3)], axis=1) for a in range(3)
    ]

    def conv(c, carry):
        total = jnp.zeros((384, 64), F32)
        for a in range(3):
            total += dot(wide[pl.ds(8 * (c + a), 8)].reshape(384, 192), forward[a], NT)
        second[pl.ds(8 * c, 8)] = total.reshape(8, 48, 64)
        return carry

    lax.fori_loop(0, 6, conv, 0)

    strips_on(choice, rows, a_recv, tile_sems.at[0], b_send, b_recv, tile_sems.at[1], me)

    for side in range(4):
        turns[0, side] = turn_matrix(side, seam[1, side, me], seam[2, side, me], False)

    head = head_ref[...]
    high = head.astype(BF16)
    rest = head - high.astype(F32)
    middle = rest.astype(BF16)
    low = (rest - middle.astype(F32)).astype(BF16)
    zero_rows = jnp.zeros((5, 64), F32)
    heads = jnp.concatenate(
        [high.astype(F32), middle.astype(F32), low.astype(F32), zero_rows], axis=0
    ).astype(BF16)

    def clear(c, carry):
        deep_wide[pl.ds(8 * c, 8)] = jnp.zeros((8, 64, 192), BF16)
        deep_wide[pl.ds(64 + 8 * c, 8)] = jnp.zeros((8, 64, 192), BF16)
        return carry

    lax.fori_loop(0, 2, clear, 0)
    shallow[0:8] = jnp.zeros((8, 48, 64), BF16)
    shallow[56:64] = jnp.zeros((8, 48, 64), BF16)

    rims = strips_in(turns.at[0], rows, b_recv, tile_sems.at[1])
    edge = jnp.zeros((8, 8, 64), F32)
    for side, a in ((0, 0), (1, 2)):
        rim = rims[side].reshape(8, 48, 64)
        shifted = jnp.concatenate(
            [
                jnp.concatenate([edge, rim[:, 0:40]], axis=1),
                rim,
                jnp.concatenate([rim[:, 8:48], edge], axis=1),
            ],
            axis=2,
        )
        extra = dot(shifted.reshape(384, 192).astype(BF16), forward[a], NT)
        second[20 * a : 20 * a + 8] += extra.reshape(8, 48, 64)
    for side, b in ((2, 0), (3, 2)):
        rim = jnp.concatenate([edge, rims[side].reshape(48, 8, 64), edge], axis=0)
        extra = jnp.zeros((384, 64), F32)
        for a in range(3):
            extra += dot(rim[8 * a : 8 * a + 48].reshape(384, 64).astype(BF16), conv_w[3 * a + b], NT)
        second[:, 20 * b : 20 * b + 8, :] += extra.reshape(48, 8, 64)

    def squash(c, carry):
        total = second[pl.ds(8 * c, 8)].reshape(384, 64)
        s = (total * jax.nn.sigmoid(total)).astype(BF16)
        act[c] = s
        lat[c, level] = dot(down, s, NT).astype(BF16)
        level_start(lat, c, lat_sems, level)
        return carry

    lax.fori_loop(0, 6, squash, 0)

    def top_step(c, carry):
        arrived_all(lat.at[c], LEVS - 1, lat_sems.at[c, 1])
        mixed = mix_ref[level, 0] * lat[c, 0].astype(F32)
        for other in range(1, LEVS):
            mixed += mix_ref[level, other] * lat[c, other].astype(F32)
        mixed = mixed.astype(BF16).astype(F32).T.astype(BF16)
        third = act[c].astype(F32) + dot(mixed, up_t)
        cot = jnp.broadcast_to(cot_ref[c].astype(F32), (8, 384)).T.astype(BF16)
        gradient = dot(cot, heads) * dsilu(third)
        top[c] = gradient
        glat[c, level] = dot(up_t, gradient.astype(BF16), NT).astype(BF16)
        level_start(glat, c, glat_sems, level)
        return carry


    lax.fori_loop(0, 6, top_step, 0)

    def deep_step(c, carry):
        arrived_all(glat.at[c], LEVS - 1, glat_sems.at[c, 1])
        mixed = mix_ref[0, level] * glat[c, 0].astype(F32)
        for other in range(1, LEVS):
            mixed += mix_ref[other, level] * glat[c, other].astype(F32)
        mixed = mixed.astype(BF16).astype(F32).T.astype(BF16)
        gradient = top[c] + dot(mixed, down)
        d = (gradient * dsilu(second[pl.ds(8 * c, 8)].reshape(384, 64))).reshape(8, 48, 64)
        z8 = jnp.zeros((8, 8, 64), F32)
        z16 = jnp.zeros((8, 16, 64), F32)
        joined = jnp.concatenate(
            [
                jnp.concatenate([d, z16], axis=1),
                jnp.concatenate([z8, d, z8], axis=1),
                jnp.concatenate([z16, d], axis=1),
            ],
            axis=2,
        )
        deep_wide[pl.ds(8 * c + 16, 8)] = joined.astype(BF16)
        return carry

    lax.fori_loop(0, 6, deep_step, 0)
    backward = [conv_w[3 * a : 3 * a + 3].reshape(192, 64) for a in range(3)]

    grad[0:8] = dot(deep_wide[16:24].reshape(512, 192), backward[0]).reshape(8, 64, 64)
    grad[56:64] = dot(deep_wide[56:64].reshape(512, 192), backward[2]).reshape(8, 64, 64)
    for near, far, take in ((0, 0, 0), (48, 56, 8)):
        total = jnp.zeros((768, 64), F32)
        for a in range(3):
            start = 8 * (3 - a)
            total += dot(deep_wide[start : start + 48, near : near + 16, :].reshape(768, 192), backward[a])
        grad[8:56, far : far + 8, :] = total.reshape(48, 16, 64)[:, take : take + 8]
    strips_out(
        edges_of(grad, [(0, 8), (56, 8), (8, 0), (8, 56)]), rows, c_send, c_recv, tile_sems.at[2], me
    )

    def adjoint(c, carry):
        total = jnp.zeros((512, 64), F32)
        for a in range(3):
            total += dot(deep_wide[pl.ds(8 * (c + 2 - a), 8)].reshape(512, 192), backward[a])
        grad[pl.ds(8 * c, 8), 8:56, :] = total.reshape(8, 64, 64)[:, 8:56]
        return carry

    lax.fori_loop(1, 7, adjoint, 0)

    def slope(c, carry):
        pre_t[pl.ds(8 * c, 8)] = dsilu(pre_t[pl.ds(8 * c, 8)])
        return carry

    lax.fori_loop(0, 6, slope, 0)
    cell = iota((8, 2304), 1)
    row = jnp.zeros((8, 2304), jnp.int32)
    for i in range(1, 48):
        row += jnp.where(cell >= 48 * i, 1, 0)
    column = cell - 48 * row
    for side in range(4):
        edge, flip = seam[1, side, me], seam[2, side, me]
        a, b = [(row, column), (47 - row, column), (column, row), (47 - column, row)][side]
        turned = 1 - lax.rem(edge, 2)
        by_rows = jnp.where(edge < 2, 1, 0)
        depth = turned * 3 + (1 - 2 * turned) * a
        along = flip * 47 + (1 - 2 * flip) * b
        index = depth * (1 + 47 * by_rows) + along * (4 - 3 * by_rows)
        index = jnp.where(a < 4, index, -1)

        def put(k, carry, side=side, index=index):
            base = pl.multiple_of(16 * k, 16)
            low_half = jnp.where(index == iota((8, 2304), 0) + base, 1.0, 0.0)
            high_half = jnp.where(index == iota((8, 2304), 0) + base + 8, 1.0, 0.0)
            place[pl.ds(pl.multiple_of(192 * side + base, 16), 16), :] = jnp.concatenate(
                [low_half, high_half], axis=0
            ).astype(BF16)
            return carry

        lax.fori_loop(0, 12, put, 0)

    strips_on(choice, rows, c_recv, tile_sems.at[2], d_send, d_recv, tile_sems.at[3], me)
    for side in range(4):
        turns[1, side] = turn_matrix(side, seam[1, side, me], seam[2, side, me], True)
    rims = strips_in(turns.at[1], rows, d_recv, tile_sems.at[3])
    grad[8:16, 8:56, :] += rims[0].reshape(8, 48, 64)
    grad[48:56, 8:56, :] += rims[1].reshape(8, 48, 64)
    grad[8:56, 8:16, :] += rims[2].reshape(48, 8, 64)
    grad[8:56, 48:56, :] += rims[3].reshape(48, 8, 64)

    def shallow_step(c, carry):
        shallow[pl.ds(8 * c + 8, 8)] = (
            grad[pl.ds(8 * c + 8, 8), 8:56, :] * pre_t[pl.ds(8 * c, 8)]
        ).astype(BF16)
        return carry

    lax.fori_loop(0, 6, shallow_step, 0)
    blank = jnp.zeros((122, 64), F32)
    inner = [
        jnp.concatenate([in_w[3 * a + b].astype(F32) for b in range(3)] + [blank], axis=0).astype(BF16)
        for a in range(3)
    ]
    for c in range(7):
        total = jnp.zeros((384, 128), F32)
        for a in range(3):
            total += dot(shallow[8 * c + 8 - 4 * a : 8 * c + 16 - 4 * a].reshape(384, 64), inner[a], NT)
        bands_t[:, 384 * c : 384 * c + 384] = total.T[0:8]
    taps = bands_t[...]
    centre, left, right = taps[2:4], taps[0:2], taps[4:6]
    position = iota((2, 2688), 1)
    line = jnp.zeros((2, 2688), jnp.int32)
    for i in range(1, 56):
        line += jnp.where(position >= 48 * i, 1, 0)
    at = position - 48 * line
    whole = (
        centre
        + jnp.where(at < 44, pltpu.roll(left, 2684, 1), 0.0)
        + jnp.where(at >= 4, pltpu.roll(right, 4, 1), 0.0)
    )
    inside = taps[:, 192:2496].astype(BF16).astype(F32)
    stacked = jnp.concatenate([inside[:, 384 * c : 384 * c + 384] for c in range(6)], axis=0)
    lane, cell8 = iota((384, 128), 1), iota((384, 128), 0)
    half = lane // 32
    source = ((lane % 32) // 4) * 48 + lane % 4 + 44 * half
    taken = jnp.where((source == cell8) & (lane < 64), 1.0, 0.0).astype(BF16)
    sides = dot(stacked.astype(BF16), taken)
    message = [
        jnp.concatenate([whole[0:1, 0:192], whole[1:2, 0:192]], axis=1),
        jnp.concatenate([whole[0:1, 2496:2688], whole[1:2, 2496:2688]], axis=1),
        jnp.concatenate([sides[8 * c + j : 8 * c + j + 1, 0:32] for j in range(2) for c in range(6)], axis=1),
        jnp.concatenate([sides[8 * c + 4 + j : 8 * c + 5 + j, 32:64] for j in range(2) for c in range(6)], axis=1),
    ]
    message = jnp.concatenate(message, axis=0)
    depth, quarter = me // 4, lax.rem(me, 4)
    for j in range(3):
        e_send[j] = message[:, 128 * j : 128 * j + 128].astype(BF16)
        e_recv[depth, j] = message[:, 128 * j : 128 * j + 128].astype(BF16)

    def tell(i, carry):
        back = 16 - i
        half = (back + 1) // 2
        there = jnp.bitwise_and(depth + jnp.where(lax.rem(back, 2) == 1, half, 16 - half), 15)
        pltpu.make_async_remote_copy(
            e_send, e_recv.at[depth], last_sems.at[0, 0], last_sems.at[0, 1],
            device_id={"tile": 4 * there + quarter}, device_id_type=MESH,
        ).start()
        return carry

    lax.fori_loop(1, 16, tell, 0)
    row_of = iota((16, 64), 0)
    own = jnp.zeros((16, 64), jnp.int32) - 1
    for member in range(4):
        for side in range(4):
            peer = seam[0, side, 4 * depth + member]
            held = jnp.where(lax.rem(peer, 4) == quarter, (peer // 4) * 4 + seam[1, side, 4 * depth + member], -1)
            own = jnp.where(row_of == 4 * member + side, held, own)
    chosen = jnp.where(own == iota((16, 64), 1), 1.0, 0.0).astype(BF16)
    active = jnp.where(panel[me] < 6, 1.0, 0.0)
    arrived_all(e_recv, 15, last_sems.at[0, 1])
    for j in range(3):
        view = rows.reshape(3, 32, 8, 128)
        for m in range(8):
            for h in range(2):
                view[j, m, 4 * h : 4 * h + 4, :] = e_recv[2 * m + h, j].astype(F32)
        found = dot(chosen, rows[j, 0:64].astype(BF16))
        for member in range(4):
            f_send[member, j] = found[4 * member : 4 * member + 4].astype(BF16)
    f_recv[quarter] = f_send[quarter]
    for i in (3, 2, 1):
        there = jnp.bitwise_xor(quarter, i)
        pltpu.make_async_remote_copy(
            f_send.at[there], f_recv.at[quarter], last_sems.at[1, 0], last_sems.at[1, 1],
            device_id={"tile": 4 * depth + there}, device_id_type=MESH,
        ).start()
    arrived_all(f_recv, 3, last_sems.at[1, 1])
    came = []
    for j in range(3):
        part = f_recv[0, j].astype(F32)
        for member in range(1, 4):
            part += f_recv[member, j].astype(F32)
        came.append(part)
    came = jnp.concatenate(came, axis=1)
    arrived = jnp.concatenate(
        [
            jnp.concatenate([came[i : i + 1, 192 * j : 192 * j + 192] for i in range(4)], axis=1)
            for j in range(2)
        ]
        + [jnp.zeros((6, 768), F32)],
        axis=0,
    )
    added = dot(arrived.astype(BF16), place[...])
    out_ref[0, 0] = (whole[:, 192:2496] + added[0:2]) * active
    for phase, buf in enumerate((a_send, b_send, c_send, d_send)):
        for j in range(3):
            arrived_all(buf.at[j], TILES - 1, tile_sems.at[phase, j, 0])
    for c in range(6):
        arrived_all(lat.at[c], LEVS - 1, lat_sems.at[c, 0])
        arrived_all(glat.at[c], LEVS - 1, glat_sems.at[c, 0])
    arrived_all(e_recv, 15, last_sems.at[0, 0])
    arrived_all(f_send, 3, last_sems.at[1, 0])


def shards(
    pre_act, cotangent, input_weight, conv_weight, down_weight, level_mix, up_weight, head_weight, seam_list,
    tile_panel,
):
    vmem = pl.BlockSpec(memory_space=pltpu.VMEM)
    smem = pl.BlockSpec(memory_space=pltpu.SMEM)
    hbm = pl.BlockSpec(memory_space=pl.ANY)
    seam_t = jnp.transpose(seam_list, (2, 1, 0))
    pieces = pltpu.VMEM((3, TILES, 4, 128), BF16)
    return pl.pallas_call(
        kernel,
        out_shape=jax.ShapeDtypeStruct((1, 1, 2, 2304), F32),
        in_specs=[hbm, vmem, vmem, hbm, vmem, smem, vmem, vmem, smem, vmem, smem],
        out_specs=vmem,
        scratch_shapes=[
            pltpu.VMEM((48, 48, 64), F32),
            pltpu.VMEM((64, 64, 64), F32),
            pltpu.VMEM((64, 48, 192), BF16),
            pltpu.VMEM((6, 384, 64), BF16),
            pltpu.VMEM((48, 48, 64), F32),
            pltpu.VMEM((6, 384, 64), F32),
            pltpu.VMEM((80, 64, 192), BF16),
            pltpu.VMEM((64, 64, 64), F32),
            pltpu.VMEM((64, 48, 64), BF16),
            pltpu.VMEM((8, 2688), F32),
            pltpu.VMEM((2, 4, 384, 384), BF16),
            pltpu.VMEM((768, 2304), BF16),
            pltpu.VMEM((3, 256, 128), F32),
            pltpu.VMEM((256, 128), jnp.int32),
            pltpu.VMEM((256, 256), BF16),
        ]
        + [pieces] * 8
        + [
            pltpu.VMEM((3, 4, 128), BF16),
            pltpu.VMEM((16, 3, 4, 128), BF16),
            pltpu.VMEM((4, 3, 4, 128), BF16),
            pltpu.VMEM((4, 3, 4, 128), BF16),
            pltpu.VMEM((6, LEVS, 8, 384), BF16),
            pltpu.VMEM((6, LEVS, 8, 384), BF16),
            pltpu.SemaphoreType.DMA((4, 3, 2)),
            pltpu.SemaphoreType.DMA((6, 2)),
            pltpu.SemaphoreType.DMA((6, 2)),
            pltpu.SemaphoreType.DMA((2, 2)),
            pltpu.VMEM((1, 1, 64, 2304), BF16),
            pltpu.VMEM((9, 64, 64), BF16),
            pltpu.SemaphoreType.DMA((2,)),
        ],
        compiler_params=pltpu.CompilerParams(
            collective_id=0, has_side_effects=True, vmem_limit_bytes=62 * 2**20
        ),
        name="adjoint",
    )(
        pre_act, cotangent.reshape(6, 1, 384), jnp.transpose(input_weight, (0, 2, 1)), conv_weight, down_weight,
        level_mix, up_weight.T, head_weight.reshape(1, 64), seam_t, seam_t, tile_panel,
    )


def solution(mesh):
    return jax.shard_map(
        shards,
        mesh=mesh,
        in_specs=(P("tile", "lev", None, None), P("tile", "lev", None), P(), P(), P(), P(), P(), P(), P(), P()),
        out_specs=P("tile", "lev", None, None),
        check_vma=False,
    )
```

```python
import functools

import jax
import jax.numpy as jnp
from jax import lax
from jax.experimental import pallas as pl
from jax.experimental.pallas import tpu as pltpu
from jax.sharding import PartitionSpec as P

F32 = jnp.float32
BF16 = jnp.bfloat16
MESH = pl.DeviceIdType.MESH
NT = (((1,), (1,)), ((), ()))
NN = (((1,), (0,)), ((), ()))
TILES = 64
LEVS = 8


def dot(a, b, dims=NN):
    return lax.dot_general(a, b, dims, preferred_element_type=F32)


def dsilu(v):
    g = jax.nn.sigmoid(v)
    return g * (1.0 + v * (1.0 - g))


def iota(shape, axis):
    return lax.broadcasted_iota(jnp.int32, shape, axis)


def peer_at(me, i):
    back = TILES - i
    half = (back + 1) // 2
    return jnp.bitwise_and(me + jnp.where(lax.rem(back, 2) == 1, half, TILES - half), TILES - 1)


def rows_from_pieces(rows, j, pieces):
    view = rows.reshape(3, 32, 8, 128)

    def step(m, carry):
        for k in range(4):
            for h in range(2):
                view[j, 4 * m + k, 4 * h : 4 * h + 4, :] = pieces[8 * m + 2 * k + h].astype(F32)
        return carry

    lax.fori_loop(0, 8, step, 0)


def pieces_from_rows(pieces, rows, j):
    view = rows.reshape(3, 32, 8, 128)

    def step(m, carry):
        for k in range(4):
            for h in range(2):
                pieces[8 * m + 2 * k + h] = view[j, 4 * m + k, 4 * h : 4 * h + 4, :].astype(BF16)
        return carry

    lax.fori_loop(0, 8, step, 0)


def slab_to_rows(rows, j, member, slab):
    rows[j, pl.ds(member, 64, stride=4), :] = jnp.concatenate([slab[0:64], slab[64:128]], axis=1)


def slab_from_rows(rows, member):
    parts = []
    for j in range(3):
        block = rows[j, pl.ds(member, 64, stride=4), :]
        parts += [block[:, :64], block[:, 64:]]
    return jnp.concatenate(parts, axis=0)


def spread_start(send, recv, sems, me):
    recv[me] = send[me]

    def step(i, carry):
        target = peer_at(me, i)
        pltpu.make_async_remote_copy(
            send.at[target], recv.at[me], sems.at[0], sems.at[1],
            device_id={"tile": target}, device_id_type=MESH,
        ).start()
        return carry

    lax.fori_loop(1, TILES, step, 0)


def arrived_all(ref, count, sem):
    some = ref.at[pl.ds(0, count)]
    pltpu.make_async_copy(some, some, sem).wait()


def strips_out(slabs, rows, send, recv, sems, me):
    for j in range(3):
        for member in range(4):
            slab_to_rows(rows, j, member, slabs[member](j))
        pieces_from_rows(send.at[j], rows, j)
        spread_start(send.at[j], recv.at[j], sems.at[j], me)


def strips_on(choice, rows, first_recv, first_sems, send, recv, sems, me):
    for j in range(3):
        arrived_all(first_recv.at[j], TILES - 1, first_sems.at[j, 1])
        rows_from_pieces(rows, j, first_recv.at[j])
        rows[j] = dot(choice[...], rows[j].astype(BF16))
        pieces_from_rows(send.at[j], rows, j)
        spread_start(send.at[j], recv.at[j], sems.at[j], me)


def strips_in(turns, rows, recv, sems):
    for j in range(3):
        arrived_all(recv.at[j], TILES - 1, sems.at[j, 1])
        rows_from_pieces(rows, j, recv.at[j])
    return [dot(turns[side], slab_from_rows(rows, side).astype(BF16)) for side in range(4)]


def level_start(buf, sems, level):
    for i in (4, 3, 5, 2, 6, 1, 7):
        pltpu.make_async_remote_copy(
            buf.at[level], buf.at[level], sems.at[0], sems.at[1],
            device_id={"lev": jnp.bitwise_and(level + i, LEVS - 1)}, device_id_type=MESH,
        ).start()


CELLS = (384, 384, 512, 512, 512)


def load_group(ref, k, first=0):
    if k < 2:
        return ref[first + 40 * k : first + 40 * k + 8].reshape(384, 64)
    if k == 2:
        middle = slice(first + 8, first + 40)
        return jnp.concatenate(
            [ref[middle, 0:8, :].reshape(256, 64), ref[middle, 40:48, :].reshape(256, 64)], axis=0
        )
    row = first + 8 + 16 * (k - 3)
    return ref[row : row + 16, 8:40, :].reshape(512, 64)


def store_group(ref, k, value, first=0):
    if k < 2:
        ref[first + 40 * k : first + 40 * k + 8] = value.reshape(8, 48, 64)
    elif k == 2:
        ref[first + 8 : first + 40, 0:8, :] = value[0:256].reshape(32, 8, 64)
        ref[first + 8 : first + 40, 40:48, :] = value[256:512].reshape(32, 8, 64)
    else:
        row = first + 8 + 16 * (k - 3)
        ref[row : row + 16, 8:40, :] = value.reshape(16, 32, 64)


def columns_joined(d):
    edge = jnp.zeros((8, 8, 64), F32)
    return jnp.concatenate(
        [
            jnp.concatenate([d[:, 8:48], edge], axis=1),
            d,
            jnp.concatenate([edge, d[:, 0:40]], axis=1),
        ],
        axis=2,
    ).astype(BF16)


def turn_matrix(side, edge, flip, of_bands):
    if side < 2:
        r, b = iota((8, 48, 128), 0), iota((8, 48, 128), 1)
    else:
        b, r = iota((48, 8, 128), 0), iota((48, 8, 128), 1)
    r, b = r.reshape(384, 128), b.reshape(384, 128)
    turned_here = (side % 2 == 0) if not of_bands else (side % 2 == 1)
    a = 7 - r if turned_here else r
    odd = lax.rem(edge, 2)
    turned_there = odd if not of_bands else 1 - odd
    depth = turned_there * 7 + (1 - 2 * turned_there) * a
    along = flip * 47 + (1 - 2 * flip) * b
    by_rows = jnp.where(edge < 2, 1, 0)
    index = depth * (1 + 47 * by_rows) + along * (8 - 7 * by_rows)
    lanes = iota((384, 128), 1)
    return jnp.concatenate(
        [jnp.where(index == lanes + 128 * j, 1.0, 0.0).astype(BF16) for j in range(3)], axis=1
    )


def kernel(
    pre_hbm, cot_ref, in_w, conv_hbm, down_ref, mix_ref, up_ref, head_ref, seam, seam_v, panel, out_ref,
    pre_t, padded, wide, act, second, top, gain, deep, deep_wide, grad, bands, shallow, bands_t, turns, place, rows, wanted,
    choice, a_send, a_recv, b_send, b_recv, c_send, c_recv, d_send, d_recv, e_send, e_recv, f_send, f_recv, lat_a, lat_b, glat_a, glat_b,
    tile_sems, lat_sems, glat_sems, last_sems, pre_ref, conv_w, load_sems,
):
    me = lax.axis_index("tile")
    level = lax.axis_index("lev")
    load_pre = pltpu.make_async_copy(pre_hbm, pre_ref, load_sems.at[0])
    load_pre.start()
    load_conv = pltpu.make_async_copy(conv_hbm, conv_w, load_sems.at[1])
    load_conv.start()
    barrier = pltpu.get_barrier_semaphore()

    def greet(i, carry):
        pl.semaphore_signal(barrier, inc=1, device_id={"tile": peer_at(me, i)}, device_id_type=MESH)
        return carry

    lax.fori_loop(1, TILES, greet, 0)
    for i in range(1, LEVS):
        pl.semaphore_signal(barrier, inc=1, device_id={"lev": lax.rem(level + i, LEVS)}, device_id_type=MESH)

    down = down_ref[...]
    up_t = up_ref[...]

    def squash(k):
        total = load_group(second, k)
        s = (total * jax.nn.sigmoid(total)).astype(BF16)
        act[k, 0 : CELLS[k]] = s
        buf = lat_a.at[k] if k < 2 else lat_b.at[k - 2]
        buf[level] = dot(down, s, NT).astype(BF16)
        level_start(buf, lat_sems.at[k], level)

    def top_step(k):
        buf = lat_a.at[k] if k < 2 else lat_b.at[k - 2]
        arrived_all(buf, LEVS - 1, lat_sems.at[k, 1])
        mixed = mix_ref[level, 0] * buf[0].astype(F32)
        for other in range(1, LEVS):
            mixed += mix_ref[level, other] * buf[other].astype(F32)
        mixed = mixed.astype(BF16).astype(F32).T.astype(BF16)
        third = act[k, 0 : CELLS[k]].astype(F32) + dot(mixed, up_t)
        gradient = load_group(gain, k) * dsilu(third)
        top[k, 0 : CELLS[k]] = gradient
        out = glat_a.at[k] if k < 2 else glat_b.at[k - 2]
        out[level] = dot(up_t, gradient.astype(BF16), NT).astype(BF16)
        level_start(out, glat_sems.at[k], level)

    def deep_step(k):
        buf = glat_a.at[k] if k < 2 else glat_b.at[k - 2]
        arrived_all(buf, LEVS - 1, glat_sems.at[k, 1])
        mixed = mix_ref[0, level] * buf[0].astype(F32)
        for other in range(1, LEVS):
            mixed += mix_ref[other, level] * buf[other].astype(F32)
        mixed = mixed.astype(BF16).astype(F32).T.astype(BF16)
        gradient = top[k, 0 : CELLS[k]] + dot(mixed, down)
        d = gradient * dsilu(load_group(second, k))
        store_group(deep, k, d.astype(BF16).astype(F32), 8)

    load_pre.wait()
    pre_t[...] = pre_ref[0, 0].astype(F32).T.reshape(48, 48, 64)
    padded[8:56, 0:8, :] = jnp.zeros((48, 8, 64), F32)
    padded[8:56, 56:64, :] = jnp.zeros((48, 8, 64), F32)

    def first(c, carry):
        v = pre_t[pl.ds(8 * c, 8)]
        s = v * jax.nn.sigmoid(v)
        padded[pl.ds(8 * c + 8, 8), 8:56, :] = s.astype(BF16).astype(F32)
        return carry

    lax.fori_loop(0, 6, first, 0)
    pl.semaphore_wait(barrier, TILES - 1 + LEVS - 1)

    def edges_of(ref, places):
        def rows_at(r, c0):
            return lambda j: ref[r : r + 8, c0 : c0 + 48, :].reshape(384, 64)[128 * j : 128 * j + 128]

        def columns_at(r, c0):
            return lambda j: ref[r + 16 * j : r + 16 * j + 16, c0 : c0 + 8, :].reshape(128, 64)

        return [rows_at(*places[0]), rows_at(*places[1]), columns_at(*places[2]), columns_at(*places[3])]

    strips_out(
        edges_of(padded, [(8, 8), (48, 8), (8, 8), (8, 48)]), rows, a_send, a_recv, tile_sems.at[0], me
    )

    wished = (seam_v[0] * 4 + seam_v[1]).astype(F32)
    wished = jnp.concatenate([wished, jnp.zeros((4, 64), F32)], axis=0)
    wished = jnp.concatenate([wished, jnp.zeros((8, 64), F32)], axis=1).T
    for side in range(4):
        wanted[pl.ds(side, 64, stride=4), :] = jnp.broadcast_to(
            wished[0:64, side : side + 1], (64, 128)
        ).astype(jnp.int32)
    table = wanted[...]
    for j in range(2):
        choice[:, 128 * j : 128 * j + 128] = jnp.where(
            table == iota((256, 128), 1) + 128 * j, 1.0, 0.0
        ).astype(BF16)

    load_conv.wait()
    wide[0:8] = jnp.zeros((8, 48, 192), BF16)
    wide[56:64] = jnp.zeros((8, 48, 192), BF16)

    def widen(c, carry):
        x = padded[pl.ds(8 * c, 8)]
        wide[pl.ds(8 * c, 8)] = jnp.concatenate([x[:, 0:48], x[:, 8:56], x[:, 16:64]], axis=2).astype(BF16)
        return carry

    lax.fori_loop(1, 7, widen, 0)
    forward = [
        jnp.concatenate([conv_w[3 * a + b] for b in range(3)], axis=1) for a in range(3)
    ]

    def conv(c, carry):
        total = jnp.zeros((384, 64), F32)
        for a in range(3):
            total += dot(wide[pl.ds(8 * (c + a), 8)].reshape(384, 192), forward[a], NT)
        second[pl.ds(8 * c, 8)] = total.reshape(8, 48, 64)
        return carry

    lax.fori_loop(0, 6, conv, 0)

    squash(3)
    squash(4)
    head = head_ref[...]
    high = head.astype(BF16)
    rest = head - high.astype(F32)
    middle = rest.astype(BF16)
    low = (rest - middle.astype(F32)).astype(BF16)
    zero_rows = jnp.zeros((5, 64), F32)
    heads = jnp.concatenate(
        [high.astype(F32), middle.astype(F32), low.astype(F32), zero_rows], axis=0
    ).astype(BF16)

    def scale(c, carry):
        cot = jnp.broadcast_to(cot_ref[c].astype(F32), (8, 384)).T.astype(BF16)
        gain[pl.ds(8 * c, 8)] = dot(cot, heads).reshape(8, 48, 64)
        return carry

    lax.fori_loop(0, 6, scale, 0)
    strips_on(choice, rows, a_recv, tile_sems.at[0], b_send, b_recv, tile_sems.at[1], me)

    for side in range(4):
        turns[0, side] = turn_matrix(side, seam[1, side, me], seam[2, side, me], False)

    top_step(3)
    top_step(4)
    deep[0:8] = jnp.zeros((8, 48, 64), F32)
    deep[56:64] = jnp.zeros((8, 48, 64), F32)
    deep_wide[0:8] = jnp.zeros((8, 48, 192), BF16)
    deep_wide[56:64] = jnp.zeros((8, 48, 192), BF16)
    shallow[0:8] = jnp.zeros((8, 48, 64), BF16)
    shallow[56:64] = jnp.zeros((8, 48, 64), BF16)
    deep_step(3)
    deep_step(4)
    rims = strips_in(turns.at[0], rows, b_recv, tile_sems.at[1])
    edge = jnp.zeros((8, 8, 64), F32)
    for side, a in ((0, 0), (1, 2)):
        rim = rims[side].reshape(8, 48, 64)
        shifted = jnp.concatenate(
            [
                jnp.concatenate([edge, rim[:, 0:40]], axis=1),
                rim,
                jnp.concatenate([rim[:, 8:48], edge], axis=1),
            ],
            axis=2,
        )
        extra = dot(shifted.reshape(384, 192).astype(BF16), forward[a], NT)
        second[20 * a : 20 * a + 8] += extra.reshape(8, 48, 64)
    for side, b in ((2, 0), (3, 2)):
        rim = jnp.concatenate([edge, rims[side].reshape(48, 8, 64), edge], axis=0)
        extra = jnp.zeros((384, 64), F32)
        for a in range(3):
            extra += dot(rim[8 * a : 8 * a + 48].reshape(384, 64).astype(BF16), conv_w[3 * a + b], NT)
        second[:, 20 * b : 20 * b + 8, :] += extra.reshape(48, 8, 64)

    for k in range(3):
        squash(k)
    for k in range(3):
        top_step(k)
    for k in range(3):
        deep_step(k)
    backward = [conv_w[3 * a : 3 * a + 3].reshape(192, 64) for a in range(3)]
    bands[0] = dot(columns_joined(deep[8:16]).reshape(384, 192), backward[0])
    bands[1] = dot(columns_joined(deep[48:56]).reshape(384, 192), backward[2])
    for side, b in ((2, 0), (3, 2)):
        total = jnp.zeros((384, 64), F32)
        for a in range(3):
            here = deep[16 - 8 * a : 64 - 8 * a, 20 * b : 20 * b + 8, :].reshape(384, 64)
            total += dot(here.astype(BF16), conv_w[3 * a + b])
        bands[side] = total
    strips_out(
        [lambda j, side=side: bands[side, 128 * j : 128 * j + 128] for side in range(4)],
        rows, c_send, c_recv, tile_sems.at[2], me,
    )

    def spread(c, carry):
        deep_wide[pl.ds(8 * c + 8, 8)] = columns_joined(deep[pl.ds(8 * c + 8, 8)])
        return carry

    lax.fori_loop(0, 6, spread, 0)

    def adjoint(c, carry):
        total = jnp.zeros((384, 64), F32)
        for a in range(3):
            total += dot(deep_wide[pl.ds(8 * (c + 2 - a), 8)].reshape(384, 192), backward[a])
        grad[pl.ds(8 * c, 8)] = total.reshape(8, 48, 64)
        return carry

    lax.fori_loop(0, 6, adjoint, 0)

    def slope(c, carry):
        pre_t[pl.ds(8 * c, 8)] = dsilu(pre_t[pl.ds(8 * c, 8)])
        return carry

    lax.fori_loop(0, 6, slope, 0)
    cell = iota((8, 2304), 1)
    row = jnp.zeros((8, 2304), jnp.int32)
    for i in range(1, 48):
        row += jnp.where(cell >= 48 * i, 1, 0)
    column = cell - 48 * row
    for side in range(4):
        edge, flip = seam[1, side, me], seam[2, side, me]
        a, b = [(row, column), (47 - row, column), (column, row), (47 - column, row)][side]
        turned = 1 - lax.rem(edge, 2)
        by_rows = jnp.where(edge < 2, 1, 0)
        depth = turned * 3 + (1 - 2 * turned) * a
        along = flip * 47 + (1 - 2 * flip) * b
        index = depth * (1 + 47 * by_rows) + along * (4 - 3 * by_rows)
        index = jnp.where(a < 4, index, -1)

        def put(k, carry, side=side, index=index):
            base = pl.multiple_of(16 * k, 16)
            low_half = jnp.where(index == iota((8, 2304), 0) + base, 1.0, 0.0)
            high_half = jnp.where(index == iota((8, 2304), 0) + base + 8, 1.0, 0.0)
            place[pl.ds(pl.multiple_of(192 * side + base, 16), 16), :] = jnp.concatenate(
                [low_half, high_half], axis=0
            ).astype(BF16)
            return carry

        lax.fori_loop(0, 12, put, 0)

    strips_on(choice, rows, c_recv, tile_sems.at[2], d_send, d_recv, tile_sems.at[3], me)
    for side in range(4):
        turns[1, side] = turn_matrix(side, seam[1, side, me], seam[2, side, me], True)
    rims = strips_in(turns.at[1], rows, d_recv, tile_sems.at[3])
    grad[0:8] += rims[0].reshape(8, 48, 64)
    grad[40:48] += rims[1].reshape(8, 48, 64)
    grad[:, 0:8, :] += rims[2].reshape(48, 8, 64)
    grad[:, 40:48, :] += rims[3].reshape(48, 8, 64)

    def shallow_step(c, carry):
        shallow[pl.ds(8 * c + 8, 8)] = (
            grad[pl.ds(8 * c, 8)] * pre_t[pl.ds(8 * c, 8)]
        ).astype(BF16)
        return carry

    lax.fori_loop(0, 6, shallow_step, 0)
    blank = jnp.zeros((122, 64), F32)
    inner = [
        jnp.concatenate([in_w[3 * a + b].astype(F32) for b in range(3)] + [blank], axis=0).astype(BF16)
        for a in range(3)
    ]
    for c in range(7):
        total = jnp.zeros((384, 128), F32)
        for a in range(3):
            total += dot(shallow[8 * c + 8 - 4 * a : 8 * c + 16 - 4 * a].reshape(384, 64), inner[a], NT)
        bands_t[:, 384 * c : 384 * c + 384] = total.T[0:8]
    taps = bands_t[...]
    centre, left, right = taps[2:4], taps[0:2], taps[4:6]
    position = iota((2, 2688), 1)
    line = jnp.zeros((2, 2688), jnp.int32)
    for i in range(1, 56):
        line += jnp.where(position >= 48 * i, 1, 0)
    at = position - 48 * line
    whole = (
        centre
        + jnp.where(at < 44, pltpu.roll(left, 2684, 1), 0.0)
        + jnp.where(at >= 4, pltpu.roll(right, 4, 1), 0.0)
    )
    inside = taps[:, 192:2496].astype(BF16).astype(F32)
    stacked = jnp.concatenate([inside[:, 384 * c : 384 * c + 384] for c in range(6)], axis=0)
    lane, cell8 = iota((384, 128), 1), iota((384, 128), 0)
    half = lane // 32
    source = ((lane % 32) // 4) * 48 + lane % 4 + 44 * half
    taken = jnp.where((source == cell8) & (lane < 64), 1.0, 0.0).astype(BF16)
    sides = dot(stacked.astype(BF16), taken)
    message = [
        jnp.concatenate([whole[0:1, 0:192], whole[1:2, 0:192]], axis=1),
        jnp.concatenate([whole[0:1, 2496:2688], whole[1:2, 2496:2688]], axis=1),
        jnp.concatenate([sides[8 * c + j : 8 * c + j + 1, 0:32] for j in range(2) for c in range(6)], axis=1),
        jnp.concatenate([sides[8 * c + 4 + j : 8 * c + 5 + j, 32:64] for j in range(2) for c in range(6)], axis=1),
    ]
    message = jnp.concatenate(message, axis=0)
    depth, quarter = me // 4, lax.rem(me, 4)
    for j in range(3):
        e_send[j] = message[:, 128 * j : 128 * j + 128].astype(BF16)
        e_recv[depth, j] = message[:, 128 * j : 128 * j + 128].astype(BF16)

    def tell(i, carry):
        back = 16 - i
        half = (back + 1) // 2
        there = jnp.bitwise_and(depth + jnp.where(lax.rem(back, 2) == 1, half, 16 - half), 15)
        pltpu.make_async_remote_copy(
            e_send, e_recv.at[depth], last_sems.at[0, 0], last_sems.at[0, 1],
            device_id={"tile": 4 * there + quarter}, device_id_type=MESH,
        ).start()
        return carry

    lax.fori_loop(1, 16, tell, 0)
    row_of = iota((16, 64), 0)
    own = jnp.zeros((16, 64), jnp.int32) - 1
    for member in range(4):
        for side in range(4):
            peer = seam[0, side, 4 * depth + member]
            held = jnp.where(lax.rem(peer, 4) == quarter, (peer // 4) * 4 + seam[1, side, 4 * depth + member], -1)
            own = jnp.where(row_of == 4 * member + side, held, own)
    chosen = jnp.where(own == iota((16, 64), 1), 1.0, 0.0).astype(BF16)
    active = jnp.where(panel[me] < 6, 1.0, 0.0)
    arrived_all(e_recv, 15, last_sems.at[0, 1])
    for j in range(3):
        view = rows.reshape(3, 32, 8, 128)
        for m in range(8):
            for h in range(2):
                view[j, m, 4 * h : 4 * h + 4, :] = e_recv[2 * m + h, j].astype(F32)
        found = dot(chosen, rows[j, 0:64].astype(BF16))
        for member in range(4):
            f_send[member, j] = found[4 * member : 4 * member + 4].astype(BF16)
    f_recv[quarter] = f_send[quarter]
    for i in (3, 2, 1):
        there = jnp.bitwise_xor(quarter, i)
        pltpu.make_async_remote_copy(
            f_send.at[there], f_recv.at[quarter], last_sems.at[1, 0], last_sems.at[1, 1],
            device_id={"tile": 4 * depth + there}, device_id_type=MESH,
        ).start()
    arrived_all(f_recv, 3, last_sems.at[1, 1])
    came = []
    for j in range(3):
        part = f_recv[0, j].astype(F32)
        for member in range(1, 4):
            part += f_recv[member, j].astype(F32)
        came.append(part)
    came = jnp.concatenate(came, axis=1)
    arrived = jnp.concatenate(
        [
            jnp.concatenate([came[i : i + 1, 192 * j : 192 * j + 192] for i in range(4)], axis=1)
            for j in range(2)
        ]
        + [jnp.zeros((6, 768), F32)],
        axis=0,
    )
    added = dot(arrived.astype(BF16), place[...])
    out_ref[0, 0] = (whole[:, 192:2496] + added[0:2]) * active
    for phase, buf in enumerate((a_send, b_send, c_send, d_send)):
        for j in range(3):
            arrived_all(buf.at[j], TILES - 1, tile_sems.at[phase, j, 0])
    for k in range(5):
        arrived_all(lat_a.at[k] if k < 2 else lat_b.at[k - 2], LEVS - 1, lat_sems.at[k, 0])
        arrived_all(glat_a.at[k] if k < 2 else glat_b.at[k - 2], LEVS - 1, glat_sems.at[k, 0])
    arrived_all(e_recv, 15, last_sems.at[0, 0])
    arrived_all(f_send, 3, last_sems.at[1, 0])


def shards(
    pre_act, cotangent, input_weight, conv_weight, down_weight, level_mix, up_weight, head_weight, seam_list,
    tile_panel,
):
    vmem = pl.BlockSpec(memory_space=pltpu.VMEM)
    smem = pl.BlockSpec(memory_space=pltpu.SMEM)
    hbm = pl.BlockSpec(memory_space=pl.ANY)
    seam_t = jnp.transpose(seam_list, (2, 1, 0))
    pieces = pltpu.VMEM((3, TILES, 4, 128), BF16)
    return pl.pallas_call(
        kernel,
        out_shape=jax.ShapeDtypeStruct((1, 1, 2, 2304), F32),
        in_specs=[hbm, vmem, vmem, hbm, vmem, smem, vmem, vmem, smem, vmem, smem],
        out_specs=vmem,
        scratch_shapes=[
            pltpu.VMEM((48, 48, 64), F32),
            pltpu.VMEM((64, 64, 64), F32),
            pltpu.VMEM((64, 48, 192), BF16),
            pltpu.VMEM((5, 512, 64), BF16),
            pltpu.VMEM((48, 48, 64), F32),
            pltpu.VMEM((5, 512, 64), F32),
            pltpu.VMEM((48, 48, 64), F32),
            pltpu.VMEM((64, 48, 64), F32),
            pltpu.VMEM((64, 48, 192), BF16),
            pltpu.VMEM((48, 48, 64), F32),
            pltpu.VMEM((4, 384, 64), F32),
            pltpu.VMEM((64, 48, 64), BF16),
            pltpu.VMEM((8, 2688), F32),
            pltpu.VMEM((2, 4, 384, 384), BF16),
            pltpu.VMEM((768, 2304), BF16),
            pltpu.VMEM((3, 256, 128), F32),
            pltpu.VMEM((256, 128), jnp.int32),
            pltpu.VMEM((256, 256), BF16),
        ]
        + [pieces] * 8
        + [
            pltpu.VMEM((3, 4, 128), BF16),
            pltpu.VMEM((16, 3, 4, 128), BF16),
            pltpu.VMEM((4, 3, 4, 128), BF16),
            pltpu.VMEM((4, 3, 4, 128), BF16),
            pltpu.VMEM((2, LEVS, 8, 384), BF16),
            pltpu.VMEM((3, LEVS, 8, 512), BF16),
            pltpu.VMEM((2, LEVS, 8, 384), BF16),
            pltpu.VMEM((3, LEVS, 8, 512), BF16),
            pltpu.SemaphoreType.DMA((4, 3, 2)),
            pltpu.SemaphoreType.DMA((5, 2)),
            pltpu.SemaphoreType.DMA((5, 2)),
            pltpu.SemaphoreType.DMA((2, 2)),
            pltpu.VMEM((1, 1, 64, 2304), BF16),
            pltpu.VMEM((9, 64, 64), BF16),
            pltpu.SemaphoreType.DMA((2,)),
        ],
        compiler_params=pltpu.CompilerParams(
            collective_id=0, has_side_effects=True, vmem_limit_bytes=62 * 2**20
        ),
        name="adjoint",
    )(
        pre_act, cotangent.reshape(6, 1, 384), jnp.transpose(input_weight, (0, 2, 1)), conv_weight, down_weight,
        level_mix, up_weight.T, head_weight.reshape(1, 64), seam_t, seam_t, tile_panel,
    )


def solution(mesh):
    return jax.shard_map(
        shards,
        mesh=mesh,
        in_specs=(P("tile", "lev", None, None), P("tile", "lev", None), P(), P(), P(), P(), P(), P(), P(), P()),
        out_specs=P("tile", "lev", None, None),
        check_vma=False,
    )
```

```python
import functools

import jax
import jax.numpy as jnp
from jax import lax
from jax.experimental import pallas as pl
from jax.experimental.pallas import tpu as pltpu
from jax.sharding import PartitionSpec as P

F32 = jnp.float32
BF16 = jnp.bfloat16
MESH = pl.DeviceIdType.MESH
NT = (((1,), (1,)), ((), ()))
NN = (((1,), (0,)), ((), ()))
TILES = 64
LEVS = 8


def dot(a, b, dims=NN):
    return lax.dot_general(a, b, dims, preferred_element_type=F32)


def dsilu(v):
    g = jax.nn.sigmoid(v)
    return g * (1.0 + v * (1.0 - g))


def iota(shape, axis):
    return lax.broadcasted_iota(jnp.int32, shape, axis)


def peer_at(me, i):
    back = TILES - i
    half = (back + 1) // 2
    return jnp.bitwise_and(me + jnp.where(lax.rem(back, 2) == 1, half, TILES - half), TILES - 1)


def rows_from_pieces(rows, j, pieces):
    view = rows.reshape(3, 32, 8, 128)

    def step(m, carry):
        for k in range(4):
            for h in range(2):
                view[j, 4 * m + k, 4 * h : 4 * h + 4, :] = pieces[8 * m + 2 * k + h].astype(F32)
        return carry

    lax.fori_loop(0, 8, step, 0)


def pieces_from_rows(pieces, rows, j):
    view = rows.reshape(3, 32, 8, 128)

    def step(m, carry):
        for k in range(4):
            for h in range(2):
                pieces[8 * m + 2 * k + h] = view[j, 4 * m + k, 4 * h : 4 * h + 4, :].astype(BF16)
        return carry

    lax.fori_loop(0, 8, step, 0)


def slab_to_rows(rows, j, member, slab):
    rows[j, pl.ds(member, 64, stride=4), :] = jnp.concatenate([slab[0:64], slab[64:128]], axis=1)


def spread_start(send, recv, sems, me):
    recv[me] = send[me]

    def step(i, carry):
        for k in range(1, 4):
            target = peer_at(me, 3 * i + k)
            pltpu.make_async_remote_copy(
                send.at[target], recv.at[me], sems.at[0], sems.at[1],
                device_id={"tile": target}, device_id_type=MESH,
            ).start()
        return carry

    lax.fori_loop(0, (TILES - 1) // 3, step, 0)


def arrived_all(ref, count, sem):
    some = ref.at[pl.ds(0, count)]
    pltpu.make_async_copy(some, some, sem).wait()


def strips_cut(slabs, rows, send, j):
    for member in range(4):
        slab_to_rows(rows, j, member, slabs[member](j))
    pieces_from_rows(send.at[j], rows, j)


def strips_on(choice, rows, first_recv, first_sems, send, recv, sems, me):
    for j in range(3):
        arrived_all(first_recv.at[j], TILES - 1, first_sems.at[j, 1])
        rows_from_pieces(rows, j, first_recv.at[j])
        rows[j] = dot(choice[...], rows[j].astype(BF16))
        pieces_from_rows(send.at[j], rows, j)
        spread_start(send.at[j], recv.at[j], sems.at[j], me)


def strips_in(turns, rows, rims, recv, sems):
    for j in range(3):
        arrived_all(recv.at[j], TILES - 1, sems.at[j, 1])
        rows_from_pieces(rows, j, recv.at[j])
        for side in range(4):
            block = rows[j, pl.ds(side, 64, stride=4), :]
            cells = jnp.concatenate([block[:, :64], block[:, 64:]], axis=0).astype(BF16)
            part = dot(turns[side, :, 128 * j : 128 * j + 128], cells)
            rims[side] = part if j == 0 else rims[side] + part


def level_start(buf, sems, level):
    for i in (4, 3, 5, 2, 6, 1, 7):
        pltpu.make_async_remote_copy(
            buf.at[level], buf.at[level], sems.at[0], sems.at[1],
            device_id={"lev": jnp.bitwise_and(level + i, LEVS - 1)}, device_id_type=MESH,
        ).start()


CELLS = (384, 384, 512, 512, 512)


def load_group(ref, k, first=0):
    if k < 2:
        return ref[first + 40 * k : first + 40 * k + 8].reshape(384, 64)
    if k == 2:
        middle = slice(first + 8, first + 40)
        return jnp.concatenate(
            [ref[middle, 0:8, :].reshape(256, 64), ref[middle, 40:48, :].reshape(256, 64)], axis=0
        )
    row = first + 8 + 16 * (k - 3)
    return ref[row : row + 16, 8:40, :].reshape(512, 64)


def store_group(ref, k, value, first=0):
    if k < 2:
        ref[first + 40 * k : first + 40 * k + 8] = value.reshape(8, 48, 64)
    elif k == 2:
        ref[first + 8 : first + 40, 0:8, :] = value[0:256].reshape(32, 8, 64)
        ref[first + 8 : first + 40, 40:48, :] = value[256:512].reshape(32, 8, 64)
    else:
        row = first + 8 + 16 * (k - 3)
        ref[row : row + 16, 8:40, :] = value.reshape(16, 32, 64)


def columns_joined(d):
    edge = jnp.zeros((8, 8, 64), F32)
    return jnp.concatenate(
        [
            jnp.concatenate([d[:, 8:48], edge], axis=1),
            d,
            jnp.concatenate([edge, d[:, 0:40]], axis=1),
        ],
        axis=2,
    ).astype(BF16)


def turn_matrix(side, edge, flip, of_bands):
    if side < 2:
        r, b = iota((8, 48, 128), 0), iota((8, 48, 128), 1)
    else:
        b, r = iota((48, 8, 128), 0), iota((48, 8, 128), 1)
    r, b = r.reshape(384, 128), b.reshape(384, 128)
    turned_here = (side % 2 == 0) if not of_bands else (side % 2 == 1)
    a = 7 - r if turned_here else r
    odd = lax.rem(edge, 2)
    turned_there = odd if not of_bands else 1 - odd
    depth = turned_there * 7 + (1 - 2 * turned_there) * a
    along = flip * 47 + (1 - 2 * flip) * b
    by_rows = jnp.where(edge < 2, 1, 0)
    index = depth * (1 + 47 * by_rows) + along * (8 - 7 * by_rows)
    lanes = iota((384, 128), 1)
    return jnp.concatenate(
        [jnp.where(index == lanes + 128 * j, 1.0, 0.0).astype(BF16) for j in range(3)], axis=1
    )


def kernel(
    pre_hbm, cot_ref, in_w, conv_hbm, down_ref, mix_ref, up_ref, head_ref, seam, seam_v, panel, out_ref,
    pre_t, padded, wide, act, second, top, gain, deep, deep_wide, grad, bands, rims, shallow, bands_t, turns, place, rows, wanted,
    choice, a_send, a_recv, b_send, b_recv, c_send, c_recv, d_send, d_recv, e_send, e_recv, f_send, f_recv, lat_a, lat_b, glat_a, glat_b,
    tile_sems, lat_sems, glat_sems, last_sems, pre_ref, conv_w, load_sems,
):
    me = lax.axis_index("tile")
    level = lax.axis_index("lev")
    load_pre = pltpu.make_async_copy(pre_hbm, pre_ref, load_sems.at[0])
    load_pre.start()
    load_conv = pltpu.make_async_copy(conv_hbm, conv_w, load_sems.at[1])
    load_conv.start()
    barrier = pltpu.get_barrier_semaphore()

    def greet(i, carry):
        pl.semaphore_signal(barrier, inc=1, device_id={"tile": peer_at(me, i)}, device_id_type=MESH)
        return carry

    lax.fori_loop(1, TILES, greet, 0)
    for i in range(1, LEVS):
        pl.semaphore_signal(barrier, inc=1, device_id={"lev": lax.rem(level + i, LEVS)}, device_id_type=MESH)

    down = down_ref[...]
    up_t = up_ref[...]

    def squash(k):
        total = load_group(second, k)
        s = (total * jax.nn.sigmoid(total)).astype(BF16)
        act[k, 0 : CELLS[k]] = s
        buf = lat_a.at[k] if k < 2 else lat_b.at[k - 2]
        buf[level] = dot(down, s, NT).astype(BF16)
        level_start(buf, lat_sems.at[k], level)

    def top_step(k):
        buf = lat_a.at[k] if k < 2 else lat_b.at[k - 2]
        arrived_all(buf, LEVS - 1, lat_sems.at[k, 1])
        mixed = mix_ref[level, 0] * buf[0].astype(F32)
        for other in range(1, LEVS):
            mixed += mix_ref[level, other] * buf[other].astype(F32)
        mixed = mixed.astype(BF16).astype(F32).T.astype(BF16)
        third = act[k, 0 : CELLS[k]].astype(F32) + dot(mixed, up_t)
        gradient = load_group(gain, k) * dsilu(third)
        top[k, 0 : CELLS[k]] = gradient
        out = glat_a.at[k] if k < 2 else glat_b.at[k - 2]
        out[level] = dot(up_t, gradient.astype(BF16), NT).astype(BF16)
        level_start(out, glat_sems.at[k], level)

    def deep_step(k):
        buf = glat_a.at[k] if k < 2 else glat_b.at[k - 2]
        arrived_all(buf, LEVS - 1, glat_sems.at[k, 1])
        mixed = mix_ref[0, level] * buf[0].astype(F32)
        for other in range(1, LEVS):
            mixed += mix_ref[other, level] * buf[other].astype(F32)
        mixed = mixed.astype(BF16).astype(F32).T.astype(BF16)
        gradient = top[k, 0 : CELLS[k]] + dot(mixed, down)
        d = gradient * dsilu(load_group(second, k))
        store_group(deep, k, d.astype(BF16).astype(F32), 8)

    load_pre.wait()
    pre_t[...] = pre_ref[0, 0].astype(F32).T.reshape(48, 48, 64)
    padded[8:56, 0:8, :] = jnp.zeros((48, 8, 64), F32)
    padded[8:56, 56:64, :] = jnp.zeros((48, 8, 64), F32)

    def first(c, carry):
        v = pre_t[pl.ds(8 * c, 8)]
        s = v * jax.nn.sigmoid(v)
        padded[pl.ds(8 * c + 8, 8), 8:56, :] = s.astype(BF16).astype(F32)
        return carry

    lax.fori_loop(0, 6, first, 0)
    def edges_of(ref, places):
        def rows_at(r, c0):
            return lambda j: ref[r : r + 8, c0 : c0 + 48, :].reshape(384, 64)[128 * j : 128 * j + 128]

        def columns_at(r, c0):
            return lambda j: ref[r + 16 * j : r + 16 * j + 16, c0 : c0 + 8, :].reshape(128, 64)

        return [rows_at(*places[0]), rows_at(*places[1]), columns_at(*places[2]), columns_at(*places[3])]

    sides = edges_of(padded, [(8, 8), (48, 8), (8, 8), (8, 48)])
    for j in range(3):
        strips_cut(sides, rows, a_send, j)
    pl.semaphore_wait(barrier, TILES - 1 + LEVS - 1)
    for j in range(3):
        spread_start(a_send.at[j], a_recv.at[j], tile_sems.at[0, j], me)

    wished = (seam_v[0] * 4 + seam_v[1]).astype(F32)
    wished = jnp.concatenate([wished, jnp.zeros((4, 64), F32)], axis=0)
    wished = jnp.concatenate([wished, jnp.zeros((8, 64), F32)], axis=1).T
    for side in range(4):
        wanted[pl.ds(side, 64, stride=4), :] = jnp.broadcast_to(
            wished[0:64, side : side + 1], (64, 128)
        ).astype(jnp.int32)
    table = wanted[...]
    for j in range(2):
        choice[:, 128 * j : 128 * j + 128] = jnp.where(
            table == iota((256, 128), 1) + 128 * j, 1.0, 0.0
        ).astype(BF16)

    load_conv.wait()
    wide[0:8] = jnp.zeros((8, 48, 192), BF16)
    wide[56:64] = jnp.zeros((8, 48, 192), BF16)

    def widen(c, carry):
        x = padded[pl.ds(8 * c, 8)]
        wide[pl.ds(8 * c, 8)] = jnp.concatenate([x[:, 0:48], x[:, 8:56], x[:, 16:64]], axis=2).astype(BF16)
        return carry

    lax.fori_loop(1, 7, widen, 0)
    forward = [
        jnp.concatenate([conv_w[3 * a + b] for b in range(3)], axis=1) for a in range(3)
    ]

    def conv(c, carry):
        total = jnp.zeros((384, 64), F32)
        for a in range(3):
            total += dot(wide[pl.ds(8 * (c + a), 8)].reshape(384, 192), forward[a], NT)
        second[pl.ds(8 * c, 8)] = total.reshape(8, 48, 64)
        return carry

    lax.fori_loop(0, 6, conv, 0)

    squash(3)
    squash(4)
    head = head_ref[...]
    high = head.astype(BF16)
    rest = head - high.astype(F32)
    middle = rest.astype(BF16)
    low = (rest - middle.astype(F32)).astype(BF16)
    zero_rows = jnp.zeros((5, 64), F32)
    heads = jnp.concatenate(
        [high.astype(F32), middle.astype(F32), low.astype(F32), zero_rows], axis=0
    ).astype(BF16)

    def scale(c, carry):
        cot = jnp.broadcast_to(cot_ref[c].astype(F32), (8, 384)).T.astype(BF16)
        gain[pl.ds(8 * c, 8)] = dot(cot, heads).reshape(8, 48, 64)
        return carry

    lax.fori_loop(0, 6, scale, 0)
    strips_on(choice, rows, a_recv, tile_sems.at[0], b_send, b_recv, tile_sems.at[1], me)

    for side in range(4):
        turns[0, side] = turn_matrix(side, seam[1, side, me], seam[2, side, me], False)

    top_step(3)
    top_step(4)
    deep[0:8] = jnp.zeros((8, 48, 64), F32)
    deep[56:64] = jnp.zeros((8, 48, 64), F32)
    deep_wide[0:8] = jnp.zeros((8, 48, 192), BF16)
    deep_wide[56:64] = jnp.zeros((8, 48, 192), BF16)
    shallow[0:8] = jnp.zeros((8, 48, 64), BF16)
    shallow[56:64] = jnp.zeros((8, 48, 64), BF16)
    deep_step(3)
    deep_step(4)
    strips_in(turns.at[0], rows, rims, b_recv, tile_sems.at[1])
    edge = jnp.zeros((8, 8, 64), F32)
    for side, a in ((0, 0), (1, 2)):
        rim = rims[side].reshape(8, 48, 64)
        shifted = jnp.concatenate(
            [
                jnp.concatenate([edge, rim[:, 0:40]], axis=1),
                rim,
                jnp.concatenate([rim[:, 8:48], edge], axis=1),
            ],
            axis=2,
        )
        extra = dot(shifted.reshape(384, 192).astype(BF16), forward[a], NT)
        second[20 * a : 20 * a + 8] += extra.reshape(8, 48, 64)
    for side, b in ((2, 0), (3, 2)):
        rim = jnp.concatenate([edge, rims[side].reshape(48, 8, 64), edge], axis=0)
        extra = jnp.zeros((384, 64), F32)
        for a in range(3):
            extra += dot(rim[8 * a : 8 * a + 48].reshape(384, 64).astype(BF16), conv_w[3 * a + b], NT)
        second[:, 20 * b : 20 * b + 8, :] += extra.reshape(48, 8, 64)

    for k in range(3):
        squash(k)
    for k in range(3):
        top_step(k)
    for k in range(3):
        deep_step(k)
    backward = [conv_w[3 * a : 3 * a + 3].reshape(192, 64) for a in range(3)]
    bands[0] = dot(columns_joined(deep[8:16]).reshape(384, 192), backward[0])
    bands[1] = dot(columns_joined(deep[48:56]).reshape(384, 192), backward[2])
    for side, b in ((2, 0), (3, 2)):
        total = jnp.zeros((384, 64), F32)
        for a in range(3):
            here = deep[16 - 8 * a : 64 - 8 * a, 20 * b : 20 * b + 8, :].reshape(384, 64)
            total += dot(here.astype(BF16), conv_w[3 * a + b])
        bands[side] = total
    sides = [lambda j, side=side: bands[side, 128 * j : 128 * j + 128] for side in range(4)]
    for j in range(3):
        strips_cut(sides, rows, c_send, j)
        spread_start(c_send.at[j], c_recv.at[j], tile_sems.at[2, j], me)

    def spread(c, carry):
        deep_wide[pl.ds(8 * c + 8, 8)] = columns_joined(deep[pl.ds(8 * c + 8, 8)])
        return carry

    lax.fori_loop(0, 6, spread, 0)

    def adjoint(c, carry):
        total = jnp.zeros((384, 64), F32)
        for a in range(3):
            total += dot(deep_wide[pl.ds(8 * (c + 2 - a), 8)].reshape(384, 192), backward[a])
        grad[pl.ds(8 * c, 8)] = total.reshape(8, 48, 64)
        return carry

    lax.fori_loop(0, 6, adjoint, 0)

    def slope(c, carry):
        pre_t[pl.ds(8 * c, 8)] = dsilu(pre_t[pl.ds(8 * c, 8)])
        return carry

    lax.fori_loop(0, 6, slope, 0)
    cell = iota((8, 2304), 1)
    row = jnp.zeros((8, 2304), jnp.int32)
    for i in range(1, 48):
        row += jnp.where(cell >= 48 * i, 1, 0)
    column = cell - 48 * row
    for side in range(4):
        edge, flip = seam[1, side, me], seam[2, side, me]
        a, b = [(row, column), (47 - row, column), (column, row), (47 - column, row)][side]
        turned = 1 - lax.rem(edge, 2)
        by_rows = jnp.where(edge < 2, 1, 0)
        depth = turned * 3 + (1 - 2 * turned) * a
        along = flip * 47 + (1 - 2 * flip) * b
        index = depth * (1 + 47 * by_rows) + along * (4 - 3 * by_rows)
        index = jnp.where(a < 4, index, -1)

        def put(k, carry, side=side, index=index):
            base = pl.multiple_of(16 * k, 16)
            low_half = jnp.where(index == iota((8, 2304), 0) + base, 1.0, 0.0)
            high_half = jnp.where(index == iota((8, 2304), 0) + base + 8, 1.0, 0.0)
            place[pl.ds(pl.multiple_of(192 * side + base, 16), 16), :] = jnp.concatenate(
                [low_half, high_half], axis=0
            ).astype(BF16)
            return carry

        lax.fori_loop(0, 12, put, 0)

    strips_on(choice, rows, c_recv, tile_sems.at[2], d_send, d_recv, tile_sems.at[3], me)
    for side in range(4):
        turns[1, side] = turn_matrix(side, seam[1, side, me], seam[2, side, me], True)
    strips_in(turns.at[1], rows, rims, d_recv, tile_sems.at[3])
    grad[0:8] += rims[0].reshape(8, 48, 64)
    grad[40:48] += rims[1].reshape(8, 48, 64)
    grad[:, 0:8, :] += rims[2].reshape(48, 8, 64)
    grad[:, 40:48, :] += rims[3].reshape(48, 8, 64)

    def shallow_step(c, carry):
        shallow[pl.ds(8 * c + 8, 8)] = (
            grad[pl.ds(8 * c, 8)] * pre_t[pl.ds(8 * c, 8)]
        ).astype(BF16)
        return carry

    lax.fori_loop(0, 6, shallow_step, 0)
    blank = jnp.zeros((122, 64), F32)
    inner = [
        jnp.concatenate([in_w[3 * a + b].astype(F32) for b in range(3)] + [blank], axis=0).astype(BF16)
        for a in range(3)
    ]
    for c in range(7):
        total = jnp.zeros((384, 128), F32)
        for a in range(3):
            total += dot(shallow[8 * c + 8 - 4 * a : 8 * c + 16 - 4 * a].reshape(384, 64), inner[a], NT)
        bands_t[:, 384 * c : 384 * c + 384] = total.T[0:8]
    taps = bands_t[...]
    centre, left, right = taps[2:4], taps[0:2], taps[4:6]
    position = iota((2, 2688), 1)
    line = jnp.zeros((2, 2688), jnp.int32)
    for i in range(1, 56):
        line += jnp.where(position >= 48 * i, 1, 0)
    at = position - 48 * line
    whole = (
        centre
        + jnp.where(at < 44, pltpu.roll(left, 2684, 1), 0.0)
        + jnp.where(at >= 4, pltpu.roll(right, 4, 1), 0.0)
    )
    inside = taps[:, 192:2496].astype(BF16).astype(F32)
    stacked = jnp.concatenate([inside[:, 384 * c : 384 * c + 384] for c in range(6)], axis=0)
    lane, cell8 = iota((384, 128), 1), iota((384, 128), 0)
    half = lane // 32
    source = ((lane % 32) // 4) * 48 + lane % 4 + 44 * half
    taken = jnp.where((source == cell8) & (lane < 64), 1.0, 0.0).astype(BF16)
    sides = dot(stacked.astype(BF16), taken)
    message = [
        jnp.concatenate([whole[0:1, 0:192], whole[1:2, 0:192]], axis=1),
        jnp.concatenate([whole[0:1, 2496:2688], whole[1:2, 2496:2688]], axis=1),
        jnp.concatenate([sides[8 * c + j : 8 * c + j + 1, 0:32] for j in range(2) for c in range(6)], axis=1),
        jnp.concatenate([sides[8 * c + 4 + j : 8 * c + 5 + j, 32:64] for j in range(2) for c in range(6)], axis=1),
    ]
    message = jnp.concatenate(message, axis=0)
    depth, quarter = me // 4, lax.rem(me, 4)
    for j in range(3):
        e_send[j] = message[:, 128 * j : 128 * j + 128].astype(BF16)
        e_recv[depth, j] = message[:, 128 * j : 128 * j + 128].astype(BF16)

    def tell(i, carry):
        back = 16 - i
        half = (back + 1) // 2
        there = jnp.bitwise_and(depth + jnp.where(lax.rem(back, 2) == 1, half, 16 - half), 15)
        pltpu.make_async_remote_copy(
            e_send, e_recv.at[depth], last_sems.at[0, 0], last_sems.at[0, 1],
            device_id={"tile": 4 * there + quarter}, device_id_type=MESH,
        ).start()
        return carry

    lax.fori_loop(1, 16, tell, 0)
    row_of = iota((16, 64), 0)
    own = jnp.zeros((16, 64), jnp.int32) - 1
    for member in range(4):
        for side in range(4):
            peer = seam[0, side, 4 * depth + member]
            held = jnp.where(lax.rem(peer, 4) == quarter, (peer // 4) * 4 + seam[1, side, 4 * depth + member], -1)
            own = jnp.where(row_of == 4 * member + side, held, own)
    chosen = jnp.where(own == iota((16, 64), 1), 1.0, 0.0).astype(BF16)
    active = jnp.where(panel[me] < 6, 1.0, 0.0)
    arrived_all(e_recv, 15, last_sems.at[0, 1])
    for j in range(3):
        view = rows.reshape(3, 32, 8, 128)
        for m in range(8):
            for h in range(2):
                view[j, m, 4 * h : 4 * h + 4, :] = e_recv[2 * m + h, j].astype(F32)
        found = dot(chosen, rows[j, 0:64].astype(BF16))
        for member in range(4):
            f_send[member, j] = found[4 * member : 4 * member + 4].astype(BF16)
    f_recv[quarter] = f_send[quarter]
    for i in (3, 2, 1):
        there = jnp.bitwise_xor(quarter, i)
        pltpu.make_async_remote_copy(
            f_send.at[there], f_recv.at[quarter], last_sems.at[1, 0], last_sems.at[1, 1],
            device_id={"tile": 4 * depth + there}, device_id_type=MESH,
        ).start()
    arrived_all(f_recv, 3, last_sems.at[1, 1])
    came = []
    for j in range(3):
        part = f_recv[0, j].astype(F32)
        for member in range(1, 4):
            part += f_recv[member, j].astype(F32)
        came.append(part)
    came = jnp.concatenate(came, axis=1)
    arrived = jnp.concatenate(
        [
            jnp.concatenate([came[i : i + 1, 192 * j : 192 * j + 192] for i in range(4)], axis=1)
            for j in range(2)
        ]
        + [jnp.zeros((6, 768), F32)],
        axis=0,
    )
    added = dot(arrived.astype(BF16), place[...])
    out_ref[0, 0] = (whole[:, 192:2496] + added[0:2]) * active
    for phase, buf in enumerate((a_send, b_send, c_send, d_send)):
        for j in range(3):
            arrived_all(buf.at[j], TILES - 1, tile_sems.at[phase, j, 0])
    for k in range(5):
        arrived_all(lat_a.at[k] if k < 2 else lat_b.at[k - 2], LEVS - 1, lat_sems.at[k, 0])
        arrived_all(glat_a.at[k] if k < 2 else glat_b.at[k - 2], LEVS - 1, glat_sems.at[k, 0])
    arrived_all(e_recv, 15, last_sems.at[0, 0])
    arrived_all(f_send, 3, last_sems.at[1, 0])


def shards(
    pre_act, cotangent, input_weight, conv_weight, down_weight, level_mix, up_weight, head_weight, seam_list,
    tile_panel,
):
    vmem = pl.BlockSpec(memory_space=pltpu.VMEM)
    smem = pl.BlockSpec(memory_space=pltpu.SMEM)
    hbm = pl.BlockSpec(memory_space=pl.ANY)
    seam_t = jnp.transpose(seam_list, (2, 1, 0))
    pieces = pltpu.VMEM((3, TILES, 4, 128), BF16)
    return pl.pallas_call(
        kernel,
        out_shape=jax.ShapeDtypeStruct((1, 1, 2, 2304), F32),
        in_specs=[hbm, vmem, vmem, hbm, vmem, smem, vmem, vmem, smem, vmem, smem],
        out_specs=vmem,
        scratch_shapes=[
            pltpu.VMEM((48, 48, 64), F32),
            pltpu.VMEM((64, 64, 64), F32),
            pltpu.VMEM((64, 48, 192), BF16),
            pltpu.VMEM((5, 512, 64), BF16),
            pltpu.VMEM((48, 48, 64), F32),
            pltpu.VMEM((5, 512, 64), F32),
            pltpu.VMEM((48, 48, 64), F32),
            pltpu.VMEM((64, 48, 64), F32),
            pltpu.VMEM((64, 48, 192), BF16),
            pltpu.VMEM((48, 48, 64), F32),
            pltpu.VMEM((4, 384, 64), F32),
            pltpu.VMEM((4, 384, 64), F32),
            pltpu.VMEM((64, 48, 64), BF16),
            pltpu.VMEM((8, 2688), F32),
            pltpu.VMEM((2, 4, 384, 384), BF16),
            pltpu.VMEM((768, 2304), BF16),
            pltpu.VMEM((3, 256, 128), F32),
            pltpu.VMEM((256, 128), jnp.int32),
            pltpu.VMEM((256, 256), BF16),
        ]
        + [pieces] * 8
        + [
            pltpu.VMEM((3, 4, 128), BF16),
            pltpu.VMEM((16, 3, 4, 128), BF16),
            pltpu.VMEM((4, 3, 4, 128), BF16),
            pltpu.VMEM((4, 3, 4, 128), BF16),
            pltpu.VMEM((2, LEVS, 8, 384), BF16),
            pltpu.VMEM((3, LEVS, 8, 512), BF16),
            pltpu.VMEM((2, LEVS, 8, 384), BF16),
            pltpu.VMEM((3, LEVS, 8, 512), BF16),
            pltpu.SemaphoreType.DMA((4, 3, 2)),
            pltpu.SemaphoreType.DMA((5, 2)),
            pltpu.SemaphoreType.DMA((5, 2)),
            pltpu.SemaphoreType.DMA((2, 2)),
            pltpu.VMEM((1, 1, 64, 2304), BF16),
            pltpu.VMEM((9, 64, 64), BF16),
            pltpu.SemaphoreType.DMA((2,)),
        ],
        compiler_params=pltpu.CompilerParams(
            collective_id=0, has_side_effects=True, vmem_limit_bytes=62 * 2**20
        ),
        name="adjoint",
    )(
        pre_act, cotangent.reshape(6, 1, 384), jnp.transpose(input_weight, (0, 2, 1)), conv_weight, down_weight,
        level_mix, up_weight.T, head_weight.reshape(1, 64), seam_t, seam_t, tile_panel,
    )


def solution(mesh):
    return jax.shard_map(
        shards,
        mesh=mesh,
        in_specs=(P("tile", "lev", None, None), P("tile", "lev", None), P(), P(), P(), P(), P(), P(), P(), P()),
        out_specs=P("tile", "lev", None, None),
        check_vma=False,
    )
```
